32 devices in a mesh: groups: 2 (over y), pre: 4 (over z), dec: 4 (over x, core).
Axes of the slice: x: 2, y: 2, z: 4, core: 2. Of those that a mesh axis runs over, the one named last changes fastest.
Arguments:
- page_pool: bfloat16 [256, 128, 8, 2, 128], P(('groups', 'pre'), None, 'dec'), parts along dimension 0, may hold values from -4 to 4
- page_scales: bfloat16 [256, 8, 2], P(('groups', 'pre'), 'dec'), parts along dimension 0, may hold values from 0.5 to 2
- queries: bfloat16 [2, 256, 64, 128], P(None, ('groups', 'pre'), 'dec'), parts along dimension 1, may hold values from -48 to 48
- new_entries: bfloat16 [2, 256, 8, 2, 128], P(None, ('groups', 'pre'), 'dec'), parts along dimension 1, may hold values from -13 to 13
- token_cache: bfloat16 [256, 4, 8, 2, 128], P(('groups', 'pre'), None, 'dec'), parts along dimension 0, may hold values from -4 to 4
- cache_fill: int32 [256], P(('groups', 'pre')), parts along dimension 0, may hold values from 0 to 4
- page_counts: int32 [8, 2], P(('groups', 'pre')), parts along dimension 0, may hold values from 1 to 30, as said below
- page_table: int32 [8, 2, 30], P(('groups', 'pre')), parts along dimension 0, may hold values from -1 to 127, as said below
Outputs:
- attended: bfloat16 [2, 256, 64, 128], P(None, ('groups', 'pre'), 'dec'), parts along dimension 1
The draws below stay inside these ranges and needn't reach their ends.
There are 2 independent parts, one for each index of `groups`. The reference program is written for one: setup_inputs(seed, part) draws one part's arguments, and reference() takes and returns one part's arrays. A program takes and returns all parts, laid end to end along the dimension named above; each array names one. Nothing has to cross between parts.
Inputs may be any that keep to these rules, and one draw needn't show every extreme that they name: `page_counts`: the 2 prompts of each decode group hold 32 pages together. page_table[g, q, j] for j < page_counts[g, q] is the pool row, owner index along pre times 32 plus a slot, of that page; -1 past the length. Every pool row holds exactly one page. Decode group g takes exactly 8 pages from each owner g - k (cyclic, k < 4) and none from other owners.
All inputs are finite; a program needn't handle non-finite values.
Results may differ from the reference program's by a relative error of at most 0.0021.
Values may be sent and summed in bfloat16 or wider, within the bound.
A program may use at most 128 MiB of HBM per device.

```python
import math
import jax
import jax.numpy as jnp
from jax import lax

QH = 64
KVH = 8
HD = 128
PG = 128
SAMPLES = 16
STEPS = 2
GEN = 4
P_GRP = 2
PAGES_GRP = 32
MAXPG = 30
ROWS = 32
TOTAL_ROWS = 128
POOL_ALL = 128
CAP = 8
SENDS = 4
STRIDE = 1
N_PRE = 4


def page_layout(key):
    extra_count = PAGES_GRP - P_GRP
    extra_pick = jax.random.randint(jax.random.fold_in(key, 11), (N_PRE, extra_count - 1), 0, P_GRP)
    forced = jax.random.randint(jax.random.fold_in(key, 12), (), 0, N_PRE)
    group_ids = jnp.arange(N_PRE, dtype=jnp.int32)
    extra_pick = jnp.where((group_ids == forced)[:, None], extra_pick[:, :1], extra_pick)
    extras = jnp.concatenate([extra_pick, (extra_pick[:, :1] + 1) % P_GRP], axis=1)
    prompt_ids = jnp.arange(P_GRP, dtype=jnp.int32)
    lengths = 1 + jnp.sum((extras[:, :, None] == prompt_ids[None, None, :]).astype(jnp.int32), axis=1)
    starts = jnp.cumsum(lengths, axis=1) - lengths
    order_scores = jax.random.randint(jax.random.fold_in(key, 13), (N_PRE, SENDS), 0, 1 << 20) * SENDS + jnp.arange(SENDS, dtype=jnp.int32)[None, :]
    block_offset = jnp.argsort(order_scores, axis=1).astype(jnp.int32)
    slot_scores = jax.random.randint(jax.random.fold_in(key, 14), (N_PRE, PAGES_GRP), 0, 1 << 20) * PAGES_GRP + jnp.arange(PAGES_GRP, dtype=jnp.int32)[None, :]
    slot_of = jnp.argsort(slot_scores, axis=1).astype(jnp.int32)
    positions = jnp.arange(MAXPG, dtype=jnp.int32)
    is_live = positions[None, None, :] < lengths[:, :, None]
    page_index = jnp.minimum(starts[:, :, None] + positions[None, None, :], PAGES_GRP - 1)
    blocks = page_index // CAP
    within = page_index % CAP
    offsets = jnp.take_along_axis(block_offset, blocks.reshape(N_PRE, -1), axis=1).reshape(blocks.shape)
    owners = (group_ids[:, None, None] - STRIDE * offsets) % N_PRE
    pool_slots = jnp.take(slot_of.reshape(-1), owners * PAGES_GRP + offsets * CAP + within)
    group_table = jnp.where(is_live, owners * PAGES_GRP + pool_slots, -1)
    return (lengths, group_table)


def draw_page_counts(key, part):
    lengths, group_table = page_layout(key)
    return lengths


def draw_page_table(key, part):
    lengths, group_table = page_layout(key)
    return group_table


def draw_queries(key, part):
    key = jax.random.fold_in(key, 3)
    shape = (STEPS, TOTAL_ROWS, QH, HD)
    return (3.0 * jnp.clip(jax.random.normal(key, shape, jnp.float32), -4.0, 4.0)).astype(jnp.bfloat16)


def draw_new_entries(key, part):
    key = jax.random.fold_in(key, 5)
    shape = (STEPS, TOTAL_ROWS, KVH, 2, HD)
    return jnp.clip(jax.random.normal(key, shape, jnp.float32), -4.0, 4.0).astype(jnp.bfloat16)


def with_ends(values, rng, least, high):
    extent = values.shape
    index_at = [jax.random.randint(jax.random.fold_in(rng, axis), (), 0, extent[axis]) for axis in range(len(extent))]
    values = values.at[tuple(index_at)].set(least)
    longest = extent.index(max(extent))
    index_at[longest] = (index_at[longest] + 1) % extent[longest]
    return values.at[tuple(index_at)].set(high)


def block_levels(stream_key, extent, pieces, low, largest):
    factor_of, own = 1.0, jax.random.fold_in(stream_key, 6)
    for axis_at, blocks in pieces:
        steps = jnp.exp(jax.random.uniform(jax.random.fold_in(own, axis_at), (blocks,), jnp.float32, low / len(pieces), largest / len(pieces)))
        factor_of = factor_of * jnp.repeat(steps, extent[axis_at] // blocks).reshape([-1 if axis == axis_at else 1 for axis in range(len(extent))])
    return factor_of


def noise(key, dims, width, limit, split=(), kind=jnp.bfloat16):
    array = jax.random.normal(key, dims, jnp.float32) * width
    if len(split) > 0:
        array = block_levels(key, dims, split, -0.22, 0.18) * array
    return jnp.clip(array, min=-limit, max=limit).astype(kind)


def setup_inputs(seed: int = 0, part: int = 0) -> dict:
    splits = jax.random.split(jax.random.key(seed), 9)
    part_splits = jax.random.split(jax.random.fold_in(splits[8], part), 9)
    page_pool = noise(part_splits[0], (POOL_ALL, PG, KVH, 2, HD), 1.0, 4.0, ((0, 4), (2, 4)))
    page_scales = jnp.clip(jnp.exp(math.log(2.0) - 1.3862944 * jax.random.uniform(part_splits[1], (POOL_ALL, KVH, 2), jnp.float32) ** block_levels(part_splits[1], (POOL_ALL, KVH, 2), ((0, 4), (1, 4)), -0.2, 0.2)), 0.5, 2.0).astype(jnp.bfloat16)
    queries = draw_queries(jax.random.fold_in(jax.random.fold_in(splits[8], part), 71), part)
    new_entries = draw_new_entries(jax.random.fold_in(jax.random.fold_in(splits[8], part), 71), part)
    token_cache = noise(part_splits[4], (TOTAL_ROWS, GEN, KVH, 2, HD), 1.0, 4.0, ((0, 4), (2, 4)))
    cache_fill = with_ends(jax.random.randint(part_splits[5], (TOTAL_ROWS,), 0, GEN + 1), jax.random.fold_in(part_splits[5], 1), 0, GEN).astype(jnp.int32)
    page_counts = draw_page_counts(jax.random.fold_in(jax.random.fold_in(splits[8], part), 71), part)
    page_table = draw_page_table(jax.random.fold_in(jax.random.fold_in(splits[8], part), 71), part)
    return dict(page_pool=page_pool, page_scales=page_scales, queries=queries, new_entries=new_entries, token_cache=token_cache, cache_fill=cache_fill, page_counts=page_counts, page_table=page_table)


def local_scores(grouped, cache_keys, fresh_keys, cache_fill, factor):
    cache_len = cache_keys.shape[2]
    step_count = fresh_keys.shape[1]
    cache_scores = jnp.einsum('pctsgd,psicd->pctsgi', grouped, cache_keys) * factor
    present = jnp.arange(cache_len, dtype=jnp.int32)[None, None, None, None, None, :] < cache_fill[:, None, None, :, None, None]
    cache_scores = jnp.where(present, cache_scores, -jnp.inf)
    fresh_scores = jnp.einsum('pctsgd,puscd->pctsgu', grouped, fresh_keys) * factor
    earlier = jnp.arange(step_count, dtype=jnp.int32)[:, None] >= jnp.arange(step_count, dtype=jnp.int32)[None, :]
    fresh_scores = jnp.where(earlier[None, None, :, None, None, :], fresh_scores, -jnp.inf)
    return (cache_scores, fresh_scores)

def local_terms(row_peak, cache_scores, fresh_scores, cache_values, fresh_values):
    cache_exp = jnp.exp(cache_scores - row_peak[..., None])
    fresh_exp = jnp.exp(fresh_scores - row_peak[..., None])
    denominator = lax.optimization_barrier(jnp.sum(cache_exp, axis=-1)) + lax.optimization_barrier(jnp.sum(fresh_exp, axis=-1))
    cache_weights = lax.optimization_barrier(cache_exp.astype(jnp.bfloat16)).astype(jnp.float32)
    fresh_weights = lax.optimization_barrier(fresh_exp.astype(jnp.bfloat16)).astype(jnp.float32)
    mixed = jnp.einsum('pctsgi,psicd->pctsgd', cache_weights, cache_values)
    mixed = mixed + jnp.einsum('pctsgu,puscd->pctsgd', fresh_weights, fresh_values)
    return (denominator, mixed)

def one_group(page_pool, page_scales, prompt_queries, fresh, cache, filled, lengths, group_table):
    factor = 1.0 / math.sqrt(HD)
    head_ratio = QH // KVH
    grouped = prompt_queries.astype(jnp.float32).reshape(STEPS, P_GRP, SAMPLES, KVH, head_ratio, HD).transpose(1, 3, 0, 2, 4, 5)
    cache_all = cache.astype(jnp.float32).reshape(P_GRP, SAMPLES, GEN, KVH, 2, HD)
    fresh_all = fresh.astype(jnp.float32).reshape(STEPS, P_GRP, SAMPLES, KVH, 2, HD).transpose(1, 0, 2, 3, 4, 5)
    filled = filled.reshape(P_GRP, SAMPLES)
    flat_rows = jnp.maximum(group_table, 0).reshape(-1)
    chosen = jnp.take(page_pool, flat_rows, axis=0).astype(jnp.float32).reshape(P_GRP, MAXPG, PG, KVH, 2, HD)
    chosen_scales = jnp.take(page_scales, flat_rows, axis=0).astype(jnp.float32).reshape(P_GRP, MAXPG, KVH, 2)
    live = jnp.arange(MAXPG, dtype=jnp.int32)[None, :] < lengths[:, None]
    key_scale = chosen_scales[..., 0].transpose(0, 2, 1)[:, :, None, None, None, :, None]
    prefix_scores = jnp.einsum('pctsgd,pjicd->pctsgji', grouped, chosen[..., 0, :]) * factor * key_scale
    prefix_scores = jnp.where(live[:, None, None, None, None, :, None], prefix_scores, -jnp.inf)
    cache_scores, fresh_scores = local_scores(grouped, cache_all[..., 0, :], fresh_all[..., 0, :], filled, factor)
    row_peak = jnp.maximum(lax.optimization_barrier(jnp.max(prefix_scores, axis=(-2, -1))), jnp.maximum(lax.optimization_barrier(jnp.max(cache_scores, axis=-1)), lax.optimization_barrier(jnp.max(fresh_scores, axis=-1))))
    denominator, mixed = local_terms(row_peak, cache_scores, fresh_scores, cache_all[..., 1, :], fresh_all[..., 1, :])
    prefix_exp = jnp.exp(prefix_scores - row_peak[..., None, None])
    denominator = denominator + lax.optimization_barrier(jnp.sum(prefix_exp, axis=(-2, -1)))
    prefix_weights = lax.optimization_barrier(prefix_exp.astype(jnp.bfloat16)).astype(jnp.float32)
    value_scale = chosen_scales[..., 1].transpose(0, 2, 1)[:, :, None, None, None, :, None]
    per_page = jnp.einsum('pctsgji,pjicd->pctsgjd', prefix_weights, chosen[..., 1, :])
    mixed = mixed + lax.optimization_barrier(jnp.sum(per_page * value_scale, axis=-2))
    result = (mixed / denominator[..., None]).astype(jnp.bfloat16)
    return result.transpose(2, 0, 3, 1, 4, 5).reshape(STEPS, ROWS, QH, HD)

def reference(page_pool, page_scales, queries, new_entries, token_cache, cache_fill, page_counts, page_table):

    def handle(inputs):
        prompt_queries, fresh, cache, filled, lengths, group_table = inputs
        return one_group(page_pool, page_scales, prompt_queries, fresh, cache, filled, lengths, group_table)
    stacked = (queries.reshape(STEPS, N_PRE, ROWS, QH, HD).swapaxes(0, 1), new_entries.reshape(STEPS, N_PRE, ROWS, KVH, 2, HD).swapaxes(0, 1), token_cache.reshape(N_PRE, ROWS, GEN, KVH, 2, HD), cache_fill.reshape(N_PRE, ROWS), page_counts, page_table)
    outputs = lax.map(handle, stacked)
    return outputs.swapaxes(0, 1).reshape(STEPS, TOTAL_ROWS, QH, HD)
```

```python
import functools
import math

import jax
import jax.numpy as jnp
from jax import lax
from jax.experimental import pallas as pl
from jax.experimental.pallas import tpu as pltpu
from jax.sharding import PartitionSpec as P


def local_scores(grouped, cache_keys, fresh_keys, cache_fill, factor):
    cache_len = cache_keys.shape[2]
    step_count = fresh_keys.shape[1]
    cache_scores = (
        jnp.einsum("pctsgd,psicd->pctsgi", grouped, cache_keys, preferred_element_type=jnp.float32)
        * factor
    )
    present = (
        jnp.arange(cache_len, dtype=jnp.int32)[None, None, None, None, None, :]
        < cache_fill[:, None, None, :, None, None]
    )
    cache_scores = jnp.where(present, cache_scores, -jnp.inf)
    fresh_scores = (
        jnp.einsum("pctsgd,puscd->pctsgu", grouped, fresh_keys, preferred_element_type=jnp.float32)
        * factor
    )
    earlier = (
        jnp.arange(step_count, dtype=jnp.int32)[:, None]
        >= jnp.arange(step_count, dtype=jnp.int32)[None, :]
    )
    fresh_scores = jnp.where(earlier[None, None, :, None, None, :], fresh_scores, -jnp.inf)
    return (cache_scores, fresh_scores)


def local_terms(row_peak, cache_scores, fresh_scores, cache_values, fresh_values):
    cache_exp = jnp.exp(cache_scores - row_peak[..., None])
    fresh_exp = jnp.exp(fresh_scores - row_peak[..., None])
    denominator = jnp.sum(cache_exp, axis=-1) + jnp.sum(fresh_exp, axis=-1)
    mixed = jnp.einsum(
        "pctsgi,psicd->pctsgd",
        cache_exp.astype(jnp.bfloat16),
        cache_values,
        preferred_element_type=jnp.float32,
    )
    mixed = mixed + jnp.einsum(
        "pctsgu,puscd->pctsgd",
        fresh_exp.astype(jnp.bfloat16),
        fresh_values,
        preferred_element_type=jnp.float32,
    )
    return (denominator, mixed)


def request_table(group_table, lengths, pool_rows, pre_count, capacity):
    prompts, page_most = group_table.shape
    is_live = lax.broadcasted_iota(jnp.int32, (prompts, page_most), 1) < lengths[:, None]
    flat_ids = jnp.where(is_live, group_table, 0).reshape(-1)
    flat_live = is_live.reshape(-1)
    owners = jnp.where(flat_live, flat_ids // pool_rows, -1)
    pool_slots = flat_ids % pool_rows
    owner_hit = (owners[:, None] == lax.broadcasted_iota(jnp.int32, (1, pre_count), 1)).astype(
        jnp.int32
    )
    before = jnp.cumsum(owner_hit, axis=0) - owner_hit
    owner_rank = jnp.sum(before * owner_hit, axis=1)
    rank_hit = (owner_rank[:, None] == lax.broadcasted_iota(jnp.int32, (1, capacity), 1)).astype(
        jnp.int32
    )
    wanted = owner_hit[:, :, None] * rank_hit[:, None, :]
    requests = jnp.sum(wanted * (pool_slots + 1)[:, None, None], axis=0) - 1
    return (requests, owners, owner_rank, flat_live)


def pick_pages(page_pool, page_scales, wanted):
    flat_rows = jnp.maximum(wanted, 0).reshape(-1)
    page_block = jnp.take(page_pool, flat_rows, axis=0).reshape(wanted.shape + page_pool.shape[1:])
    scale_block = jnp.take(page_scales, flat_rows, axis=0).reshape(
        wanted.shape + page_scales.shape[1:]
    )
    return (page_block, scale_block)


def move_pages(
    page_pool, page_scales, queries, new_entries, token_cache, cache_fill, page_counts, page_table
):
    pre_count = lax.axis_size("pre")
    pool_rows = page_pool.shape[0]
    capacity = max(1, pool_rows // pre_count)
    kv_count = page_pool.shape[2]
    step_count, row_count, head_count, head_width = queries.shape
    prompts = page_counts.shape[1]
    page_most = page_table.shape[2]
    samples = row_count // prompts
    cache_len = token_cache.shape[1]
    head_ratio = head_count // kv_count
    factor = 1.0 / math.sqrt(head_width)
    requests, owners, owner_rank, flat_live = request_table(
        page_table[0], page_counts[0], pool_rows, pre_count, capacity
    )
    incoming = lax.all_to_all(requests, "pre", split_axis=0, concat_axis=0, tiled=True)
    page_block, scale_block = pick_pages(page_pool, page_scales, incoming)
    arrived, arrived_scales = (
        lax.all_to_all(page_block, "pre", split_axis=0, concat_axis=0, tiled=True),
        lax.all_to_all(scale_block, "pre", split_axis=0, concat_axis=0, tiled=True),
    )
    places = owners * capacity + owner_rank
    places = jnp.where(flat_live, places, 0)
    arrived = arrived.reshape((-1,) + page_pool.shape[1:])
    arrived_scales = arrived_scales.reshape((-1,) + page_scales.shape[1:])
    grouped = queries.reshape(
        step_count, prompts, samples, kv_count, head_ratio, head_width
    ).transpose(1, 3, 0, 2, 4, 5)
    cache_all = token_cache.reshape(prompts, samples, cache_len, kv_count, 2, head_width)
    fresh_all = new_entries.reshape(
        step_count, prompts, samples, kv_count, 2, head_width
    ).transpose(1, 0, 2, 3, 4, 5)
    filled = cache_fill.reshape(prompts, samples)
    cache_values = cache_all[..., 1, :]
    fresh_values = fresh_all[..., 1, :]
    cache_scores, fresh_scores = local_scores(
        grouped, cache_all[..., 0, :], fresh_all[..., 0, :], filled, factor
    )
    page_spots = places.reshape(prompts, page_most)
    live_pages = flat_live.reshape(prompts, page_most)

    def prompt_block(inputs):
        page_spot, live_row, prompt_query, cache_part, fresh_part, cache_vals, fresh_vals = inputs
        chosen = jnp.take(arrived, page_spot, axis=0)
        chosen_scales = jnp.take(arrived_scales, page_spot, axis=0).astype(jnp.float32)
        key_scale = chosen_scales[:, :, 0].T[:, None, None, None, :, None]
        prefix_scores = (
            jnp.einsum(
                "ctsgd,jicd->ctsgji",
                prompt_query,
                chosen[:, :, :, 0, :],
                preferred_element_type=jnp.float32,
            )
            * factor
            * key_scale
        )
        prefix_scores = jnp.where(live_row[:, None], prefix_scores, -jnp.inf)
        row_peak = jnp.maximum(
            jnp.max(prefix_scores, axis=(-2, -1)),
            jnp.maximum(jnp.max(cache_part, axis=-1), jnp.max(fresh_part, axis=-1)),
        )
        denominator, mixed = local_terms(
            row_peak[None], cache_part[None], fresh_part[None], cache_vals[None], fresh_vals[None]
        )
        prefix_exp = jnp.exp(prefix_scores - row_peak[..., None, None])
        denominator = denominator[0] + jnp.sum(prefix_exp, axis=(-2, -1))
        value_scale = chosen_scales[:, :, 1].T[:, None, None, None, :, None]
        per_page = jnp.einsum(
            "ctsgji,jicd->ctsgjd",
            prefix_exp.astype(jnp.bfloat16),
            chosen[:, :, :, 1, :],
            preferred_element_type=jnp.float32,
        )
        mixed = mixed[0] + jnp.sum(per_page * value_scale, axis=-2)
        return (mixed / denominator[..., None]).astype(jnp.bfloat16)

    result = lax.map(
        prompt_block,
        (page_spots, live_pages, grouped, cache_scores, fresh_scores, cache_values, fresh_values),
    )
    return result.transpose(2, 0, 3, 1, 4, 5).reshape(step_count, row_count, head_count, head_width)


MESH = pl.DeviceIdType.MESH
LOW = -1e30
FULL = 32000.0


def partner_of(me, k, count):
    bit, result = 1, 0
    while bit < count:
        result = result + ((me // bit) % 2 + (k // bit) % 2) % 2 * bit
        bit *= 2
    return result


def request_kernel(pool_rows, counts_ref, table_ref, out_ref, rank_ref):
    for owner in range(out_ref.shape[0]):
        rank_ref[owner] = 0
    for prompt in range(table_ref.shape[1]):

        def place(j, carry, prompt=prompt):
            page = table_ref[0, prompt, j]
            owner = page // pool_rows
            rank = rank_ref[owner]
            out_ref[owner, rank] = (page - owner * pool_rows) * 2 + prompt
            rank_ref[owner] = rank + 1
            return carry

        lax.fori_loop(0, counts_ref[0, prompt], place, 0)


def nt_dot(a, b):
    return lax.dot_general(a, b, (((1,), (1,)), ((), ())), preferred_element_type=jnp.float32)


def attend_kernel(
    dims,
    request_ref,
    scale_ref,
    fill_ref,
    queries_ref,
    cache_ref,
    fresh_ref,
    pool_ref,
    out_ref,
    raw,
    keys,
    values,
    asked,
    asked_smem,
    query_slots,
    query_now,
    scores,
    sums,
    part_out,
    part_in,
    stat_out,
    stat_in,
    local_sum,
    local_stat,
    turned,
    pool_sem,
    smem_sem,
    ask_send,
    ask_recv,
    query_send,
    query_recv,
    part_send,
    part_recv,
    stat_send,
    stat_recv,
):
    count, capacity, factor = dims
    pages = raw.shape[0]
    me = lax.axis_index("pre")
    partners = [partner_of(me, k, count) for k in range(count)]

    barrier = pltpu.get_barrier_semaphore()
    for k in range(1, count):
        pl.semaphore_signal(barrier, inc=1, device_id={"pre": partners[k]}, device_id_type=MESH)
    pool_copy = pltpu.make_async_copy(pool_ref, raw, pool_sem)
    pool_copy.start()
    own_ask = pltpu.make_async_copy(request_ref.at[me], asked_smem.at[0], smem_sem.at[0])
    own_ask.start()

    for prompt in range(2):
        for step in range(2):
            block = queries_ref[step, prompt * 16 : prompt * 16 + 16].astype(jnp.float32)
            for c in range(2):
                rows = block[:, c * 8 : c * 8 + 8, :].reshape(128, 128)
                query_slots[0, c, prompt, step * 128 : step * 128 + 128, :] = rows.astype(
                    jnp.bfloat16
                )
    pl.semaphore_wait(barrier, count - 1)

    def ask_copy(k, target):
        return pltpu.make_async_remote_copy(
            src_ref=request_ref.at[target],
            dst_ref=asked.at[k],
            send_sem=ask_send.at[k],
            recv_sem=ask_recv.at[k],
            device_id={"pre": target},
            device_id_type=MESH,
        )

    def query_copy(k, c, target):
        return pltpu.make_async_remote_copy(
            src_ref=query_slots.at[0, c],
            dst_ref=query_slots.at[k, c],
            send_sem=query_send.at[k, c],
            recv_sem=query_recv.at[k, c],
            device_id={"pre": target},
            device_id_type=MESH,
        )

    def part_copy(k, c, target):
        return pltpu.make_async_remote_copy(
            src_ref=part_out.at[k, c],
            dst_ref=part_in.at[k, c],
            send_sem=part_send.at[k, c],
            recv_sem=part_recv.at[k, c],
            device_id={"pre": target},
            device_id_type=MESH,
        )

    def stat_copy(k, c, target):
        return pltpu.make_async_remote_copy(
            src_ref=stat_out.at[k, c],
            dst_ref=stat_in.at[k, c],
            send_sem=stat_send.at[k, c],
            recv_sem=stat_recv.at[k, c],
            device_id={"pre": target},
            device_id_type=MESH,
        )

    for k in range(1, count):
        ask_copy(k, partners[k]).start()
    for c in range(2):
        for k in range(1, count):
            query_copy(k, c, partners[k]).start()

    to_row = lax.broadcasted_iota(jnp.int32, (256, 256), 0)
    from_row = lax.broadcasted_iota(jnp.int32, (256, 256), 1)
    order = jnp.where(from_row == (to_row % 64) * 4 + to_row // 64, 1.0, 0.0).astype(jnp.bfloat16)

    def sort_rows(block):
        return jnp.dot(order, block, preferred_element_type=jnp.float32)

    fresh_block = jnp.concatenate(
        [
            fresh_ref[step * 128 + prompt * 64 : step * 128 + prompt * 64 + 64, :]
            for prompt in range(2)
            for step in range(2)
        ],
        axis=0,
    )
    fresh_rows = sort_rows(fresh_block)
    key_at = lax.broadcasted_iota(jnp.int32, (128, 256), 0)
    query_at = lax.broadcasted_iota(jnp.int32, (128, 256), 1)
    query_sample = (query_at // 8) % 16
    is_cache = key_at < 64
    is_fresh = (key_at >= 64) & (key_at < 96)
    fresh_ok = is_fresh & (key_at % 16 == query_sample) & ((key_at - 64) // 16 <= query_at // 128)
    cache_same = is_cache & (key_at // 4 == query_sample)
    for prompt in range(2):
        cache_rows = sort_rows(cache_ref[prompt * 256 : prompt * 256 + 256, :])
        filled = jnp.zeros((128, 256), jnp.int32)
        for sample in range(16):
            filled = jnp.where(query_sample == sample, fill_ref[prompt * 16 + sample], filled)
        present = (cache_same & (key_at % 4 < filled)) | fresh_ok
        for c in range(2):

            def pick(kind):
                at = (c * 2 + kind) * 64
                return jnp.concatenate(
                    [
                        cache_rows[at : at + 64],
                        fresh_rows[at + prompt * 32 : at + prompt * 32 + 32],
                        jnp.zeros((32, 128), jnp.float32),
                    ],
                    axis=0,
                )

            part = nt_dot(pick(0).astype(jnp.bfloat16), query_slots[0, c, prompt]) * factor
            part = jnp.where(present, part, LOW)
            peak = jnp.max(part, axis=0, keepdims=True)
            grown = jnp.exp(part - peak)
            local_stat[c, prompt, 0:1, :] = peak
            local_stat[c, prompt, 1:2, :] = jnp.sum(grown, axis=0, keepdims=True)
            local_sum[c, prompt] = jnp.dot(
                pick(1).T.astype(jnp.bfloat16),
                grown.astype(jnp.bfloat16),
                preferred_element_type=jnp.float32,
            )

    pool_copy.wait()

    def sort_page(page, carry):
        halves = [sort_rows(raw[page, h * 256 : h * 256 + 256, :]) for h in range(2)]
        for c in range(2):
            at = c * 128
            keys[page, c] = jnp.concatenate([x[at : at + 64] for x in halves], axis=0).astype(
                jnp.bfloat16
            )
            values[page, c] = jnp.concatenate(
                [x[at + 64 : at + 128] for x in halves], axis=0
            ).T.astype(jnp.bfloat16)
        return carry

    lax.fori_loop(0, pages, sort_page, 0)
    own_ask.wait()

    def serve(index, carry):
        c, k = index // count, index % count
        target = partner_of(me, k, count)

        @pl.when((c == 0) & (k > 0))
        def _():
            ask_copy(k, target).wait_recv()
            to_smem = pltpu.make_async_copy(asked.at[k], asked_smem.at[k], smem_sem.at[k])
            to_smem.start()
            to_smem.wait()

        @pl.when(k > 0)
        def _():
            query_copy(k, c, target).wait_recv()

        query_now[...] = query_slots[k, c]
        codes = [asked_smem[k, 0, j] for j in range(capacity)]
        slots = [code // 2 for code in codes]
        prompts = [code % 2 for code in codes]
        peaks = [jnp.full((1, 256), LOW, jnp.float32) for _ in range(2)]
        for j in range(capacity):
            key_scale = scale_ref[c * 2 * pages + slots[j]] * factor
            part = nt_dot(keys[slots[j], c], query_now[prompts[j]]) * key_scale
            scores[j] = part
            peak = jnp.max(part, axis=0, keepdims=True)
            for p in range(2):
                peaks[p] = jnp.maximum(peaks[p], jnp.where(prompts[j] == p, peak, LOW))
        totals = [jnp.zeros((1, 256), jnp.float32) for _ in range(2)]
        sums[...] = jnp.zeros_like(sums)
        for j in range(capacity):
            peak = jnp.where(prompts[j] == 0, peaks[0], peaks[1])
            grown = jnp.exp(scores[j] - peak)
            total = jnp.sum(grown, axis=0, keepdims=True)
            mixed = jnp.dot(
                values[slots[j], c],
                grown.astype(jnp.bfloat16),
                preferred_element_type=jnp.float32,
            )
            value_scale = scale_ref[(c * 2 + 1) * pages + slots[j]]
            for p in range(2):
                totals[p] = totals[p] + jnp.where(prompts[j] == p, total, 0.0)
                sums[p] = sums[p] + mixed * jnp.where(prompts[j] == p, value_scale, 0.0)
        for p in range(2):
            mixed = sums[p]
            largest = jnp.max(jnp.abs(mixed), axis=0, keepdims=True)
            coded = jnp.round(mixed * (FULL / jnp.maximum(largest, 1e-30)))
            part_out[k, c, p] = coded.astype(jnp.int32).astype(jnp.int16)
            stat_out[k, c, p * 4 : p * 4 + 1, :] = peaks[p]
            stat_out[k, c, p * 4 + 1 : p * 4 + 2, :] = totals[p]
            stat_out[k, c, p * 4 + 2 : p * 4 + 3, :] = largest * (1.0 / FULL)
            stat_out[k, c, p * 4 + 3 : p * 4 + 4, :] = jnp.zeros((1, 256), jnp.float32)

        @pl.when(k > 0)
        def _():
            stat_copy(k, c, target).start()
            part_copy(k, c, target).start()

        return carry

    lax.fori_loop(0, 2 * count, serve, 0)

    for c in range(2):
        for k in range(1, count):
            stat_copy(k, c, partners[k]).wait_recv()
            part_copy(k, c, partners[k]).wait_recv()
        for p in range(2):
            stats = [stat_out[0, c]] + [stat_in[k, c] for k in range(1, count)]
            parts = [part_out[0, c, p]] + [part_in[k, c, p] for k in range(1, count)]
            local_peak = local_stat[c, p, 0:1, :]
            peak = local_peak
            for stat in stats:
                peak = jnp.maximum(peak, stat[p * 4 : p * 4 + 1])
            share = jnp.exp(local_peak - peak)
            total = share * local_stat[c, p, 1:2, :]
            mixed = local_sum[c, p] * share
            for stat, part in zip(stats, parts):
                share = jnp.exp(stat[p * 4 : p * 4 + 1] - peak)
                total = total + share * stat[p * 4 + 1 : p * 4 + 2]
                weight = share * stat[p * 4 + 2 : p * 4 + 3]
                mixed = mixed + part.astype(jnp.int32).astype(jnp.float32) * weight
            turned[p, c] = (mixed / total).T.reshape(2, 16, 8, 128)
    for p in range(2):
        both = jnp.concatenate([turned[p, 0], turned[p, 1]], axis=2)
        out_ref[:, p * 16 : p * 16 + 16] = both.astype(jnp.bfloat16)

    for k in range(1, count):
        ask_copy(k, partners[k]).wait_send()
        for c in range(2):
            query_copy(k, c, partners[k]).wait_send()
            stat_copy(k, c, partners[k]).wait_send()
            part_copy(k, c, partners[k]).wait_send()


def move_queries(
    page_pool, page_scales, queries, new_entries, token_cache, cache_fill, page_counts, page_table
):
    count = lax.axis_size("pre")
    pool_rows = page_pool.shape[0]
    capacity = pool_rows // count
    width = queries.shape[-1]
    requests = pl.pallas_call(
        functools.partial(request_kernel, pool_rows),
        out_shape=jax.ShapeDtypeStruct((count, 128), jnp.int32),
        in_specs=[pl.BlockSpec(memory_space=pltpu.SMEM)] * 2,
        out_specs=pl.BlockSpec(memory_space=pltpu.SMEM),
        scratch_shapes=[pltpu.SMEM((count,), jnp.int32)],
    )(page_counts, page_table)
    scales = page_scales.transpose(1, 2, 0).reshape(-1).astype(jnp.float32)
    vmem = pl.BlockSpec(memory_space=pltpu.VMEM)
    smem = pl.BlockSpec(memory_space=pltpu.SMEM)
    dma = pltpu.SemaphoreType.DMA
    f32, bf16 = jnp.float32, jnp.bfloat16
    return pl.pallas_call(
        functools.partial(attend_kernel, (count, capacity, 1.0 / math.sqrt(width))),
        out_shape=jax.ShapeDtypeStruct(queries.shape, queries.dtype),
        in_specs=[vmem, smem, smem, vmem, vmem, vmem, pl.BlockSpec(memory_space=pl.ANY)],
        out_specs=vmem,
        scratch_shapes=[
            pltpu.VMEM((pool_rows, 512, 128), bf16),
            pltpu.VMEM((pool_rows, 2, 128, 128), bf16),
            pltpu.VMEM((pool_rows, 2, 128, 128), bf16),
            pltpu.VMEM((count, 1, 128), jnp.int32),
            pltpu.SMEM((count, 1, 128), jnp.int32),
            pltpu.VMEM((count, 2, 2, 256, 128), bf16),
            pltpu.VMEM((2, 256, 128), bf16),
            pltpu.VMEM((capacity, 128, 256), f32),
            pltpu.VMEM((2, 128, 256), f32),
            pltpu.VMEM((count, 2, 2, 128, 256), jnp.int16),
            pltpu.VMEM((count, 2, 2, 128, 256), jnp.int16),
            pltpu.VMEM((count, 2, 8, 256), f32),
            pltpu.VMEM((count, 2, 8, 256), f32),
            pltpu.VMEM((2, 2, 128, 256), f32),
            pltpu.VMEM((2, 2, 8, 256), f32),
            pltpu.VMEM((2, 2, 2, 16, 8, 128), f32),
            dma,
            dma((count,)),
            dma((count,)),
            dma((count,)),
            dma((count, 2)),
            dma((count, 2)),
            dma((count, 2)),
            dma((count, 2)),
            dma((count, 2)),
            dma((count, 2)),
        ],
        compiler_params=pltpu.CompilerParams(
            collective_id=0, has_side_effects=True, vmem_limit_bytes=40 * 1024 * 1024
        ),
    )(
        requests.reshape(count, 1, 128),
        scales,
        cache_fill,
        queries,
        token_cache.reshape(-1, width),
        new_entries.reshape(-1, width),
        page_pool.reshape(pool_rows, -1, width),
    )


def shards(
    page_pool, page_scales, queries, new_entries, token_cache, cache_fill, page_counts, page_table
):
    args = (
        page_pool, page_scales, queries, new_entries, token_cache, cache_fill, page_counts, page_table,
    )
    count = lax.axis_size("pre")
    capacity = page_pool.shape[0] // count
    if count in (2, 4, 8) and capacity * page_pool[0].size > 2 * queries.size:
        return move_queries(*args)
    return move_pages(*args)


def solution(mesh):
    in_specs = (
        P(("groups", "pre"), None, "dec", None, None),
        P(("groups", "pre"), "dec", None),
        P(None, ("groups", "pre"), "dec", None),
        P(None, ("groups", "pre"), "dec", None, None),
        P(("groups", "pre"), None, "dec", None, None),
        P(("groups", "pre")),
        P(("groups", "pre"), None),
        P(("groups", "pre"), None, None),
    )
    out_specs = P(None, ("groups", "pre"), "dec", None)
    return jax.shard_map(shards, mesh=mesh, in_specs=in_specs, out_specs=out_specs, check_vma=False)
```

```python
import functools
import math

import jax
import jax.numpy as jnp
from jax import lax
from jax.experimental import pallas as pl
from jax.experimental.pallas import tpu as pltpu
from jax.sharding import PartitionSpec as P


def local_scores(grouped, cache_keys, fresh_keys, cache_fill, factor):
    cache_len = cache_keys.shape[2]
    step_count = fresh_keys.shape[1]
    cache_scores = (
        jnp.einsum("pctsgd,psicd->pctsgi", grouped, cache_keys, preferred_element_type=jnp.float32)
        * factor
    )
    present = (
        jnp.arange(cache_len, dtype=jnp.int32)[None, None, None, None, None, :]
        < cache_fill[:, None, None, :, None, None]
    )
    cache_scores = jnp.where(present, cache_scores, -jnp.inf)
    fresh_scores = (
        jnp.einsum("pctsgd,puscd->pctsgu", grouped, fresh_keys, preferred_element_type=jnp.float32)
        * factor
    )
    earlier = (
        jnp.arange(step_count, dtype=jnp.int32)[:, None]
        >= jnp.arange(step_count, dtype=jnp.int32)[None, :]
    )
    fresh_scores = jnp.where(earlier[None, None, :, None, None, :], fresh_scores, -jnp.inf)
    return (cache_scores, fresh_scores)


def local_terms(row_peak, cache_scores, fresh_scores, cache_values, fresh_values):
    cache_exp = jnp.exp(cache_scores - row_peak[..., None])
    fresh_exp = jnp.exp(fresh_scores - row_peak[..., None])
    denominator = jnp.sum(cache_exp, axis=-1) + jnp.sum(fresh_exp, axis=-1)
    mixed = jnp.einsum(
        "pctsgi,psicd->pctsgd",
        cache_exp.astype(jnp.bfloat16),
        cache_values,
        preferred_element_type=jnp.float32,
    )
    mixed = mixed + jnp.einsum(
        "pctsgu,puscd->pctsgd",
        fresh_exp.astype(jnp.bfloat16),
        fresh_values,
        preferred_element_type=jnp.float32,
    )
    return (denominator, mixed)


def request_table(group_table, lengths, pool_rows, pre_count, capacity):
    prompts, page_most = group_table.shape
    is_live = lax.broadcasted_iota(jnp.int32, (prompts, page_most), 1) < lengths[:, None]
    flat_ids = jnp.where(is_live, group_table, 0).reshape(-1)
    flat_live = is_live.reshape(-1)
    owners = jnp.where(flat_live, flat_ids // pool_rows, -1)
    pool_slots = flat_ids % pool_rows
    owner_hit = (owners[:, None] == lax.broadcasted_iota(jnp.int32, (1, pre_count), 1)).astype(
        jnp.int32
    )
    before = jnp.cumsum(owner_hit, axis=0) - owner_hit
    owner_rank = jnp.sum(before * owner_hit, axis=1)
    rank_hit = (owner_rank[:, None] == lax.broadcasted_iota(jnp.int32, (1, capacity), 1)).astype(
        jnp.int32
    )
    wanted = owner_hit[:, :, None] * rank_hit[:, None, :]
    requests = jnp.sum(wanted * (pool_slots + 1)[:, None, None], axis=0) - 1
    return (requests, owners, owner_rank, flat_live)


def pick_pages(page_pool, page_scales, wanted):
    flat_rows = jnp.maximum(wanted, 0).reshape(-1)
    page_block = jnp.take(page_pool, flat_rows, axis=0).reshape(wanted.shape + page_pool.shape[1:])
    scale_block = jnp.take(page_scales, flat_rows, axis=0).reshape(
        wanted.shape + page_scales.shape[1:]
    )
    return (page_block, scale_block)


def move_pages(
    page_pool, page_scales, queries, new_entries, token_cache, cache_fill, page_counts, page_table
):
    pre_count = lax.axis_size("pre")
    pool_rows = page_pool.shape[0]
    capacity = max(1, pool_rows // pre_count)
    kv_count = page_pool.shape[2]
    step_count, row_count, head_count, head_width = queries.shape
    prompts = page_counts.shape[1]
    page_most = page_table.shape[2]
    samples = row_count // prompts
    cache_len = token_cache.shape[1]
    head_ratio = head_count // kv_count
    factor = 1.0 / math.sqrt(head_width)
    requests, owners, owner_rank, flat_live = request_table(
        page_table[0], page_counts[0], pool_rows, pre_count, capacity
    )
    incoming = lax.all_to_all(requests, "pre", split_axis=0, concat_axis=0, tiled=True)
    page_block, scale_block = pick_pages(page_pool, page_scales, incoming)
    arrived, arrived_scales = (
        lax.all_to_all(page_block, "pre", split_axis=0, concat_axis=0, tiled=True),
        lax.all_to_all(scale_block, "pre", split_axis=0, concat_axis=0, tiled=True),
    )
    places = owners * capacity + owner_rank
    places = jnp.where(flat_live, places, 0)
    arrived = arrived.reshape((-1,) + page_pool.shape[1:])
    arrived_scales = arrived_scales.reshape((-1,) + page_scales.shape[1:])
    grouped = queries.reshape(
        step_count, prompts, samples, kv_count, head_ratio, head_width
    ).transpose(1, 3, 0, 2, 4, 5)
    cache_all = token_cache.reshape(prompts, samples, cache_len, kv_count, 2, head_width)
    fresh_all = new_entries.reshape(
        step_count, prompts, samples, kv_count, 2, head_width
    ).transpose(1, 0, 2, 3, 4, 5)
    filled = cache_fill.reshape(prompts, samples)
    cache_values = cache_all[..., 1, :]
    fresh_values = fresh_all[..., 1, :]
    cache_scores, fresh_scores = local_scores(
        grouped, cache_all[..., 0, :], fresh_all[..., 0, :], filled, factor
    )
    page_spots = places.reshape(prompts, page_most)
    live_pages = flat_live.reshape(prompts, page_most)

    def prompt_block(inputs):
        page_spot, live_row, prompt_query, cache_part, fresh_part, cache_vals, fresh_vals = inputs
        chosen = jnp.take(arrived, page_spot, axis=0)
        chosen_scales = jnp.take(arrived_scales, page_spot, axis=0).astype(jnp.float32)
        key_scale = chosen_scales[:, :, 0].T[:, None, None, None, :, None]
        prefix_scores = (
            jnp.einsum(
                "ctsgd,jicd->ctsgji",
                prompt_query,
                chosen[:, :, :, 0, :],
                preferred_element_type=jnp.float32,
            )
            * factor
            * key_scale
        )
        prefix_scores = jnp.where(live_row[:, None], prefix_scores, -jnp.inf)
        row_peak = jnp.maximum(
            jnp.max(prefix_scores, axis=(-2, -1)),
            jnp.maximum(jnp.max(cache_part, axis=-1), jnp.max(fresh_part, axis=-1)),
        )
        denominator, mixed = local_terms(
            row_peak[None], cache_part[None], fresh_part[None], cache_vals[None], fresh_vals[None]
        )
        prefix_exp = jnp.exp(prefix_scores - row_peak[..., None, None])
        denominator = denominator[0] + jnp.sum(prefix_exp, axis=(-2, -1))
        value_scale = chosen_scales[:, :, 1].T[:, None, None, None, :, None]
        per_page = jnp.einsum(
            "ctsgji,jicd->ctsgjd",
            prefix_exp.astype(jnp.bfloat16),
            chosen[:, :, :, 1, :],
            preferred_element_type=jnp.float32,
        )
        mixed = mixed[0] + jnp.sum(per_page * value_scale, axis=-2)
        return (mixed / denominator[..., None]).astype(jnp.bfloat16)

    result = lax.map(
        prompt_block,
        (page_spots, live_pages, grouped, cache_scores, fresh_scores, cache_values, fresh_values),
    )
    return result.transpose(2, 0, 3, 1, 4, 5).reshape(step_count, row_count, head_count, head_width)


MESH = pl.DeviceIdType.MESH
LOW = -1e30
FULL = 32000.0


def partner_of(me, k, count):
    bit, result = 1, 0
    while bit < count:
        result = result + ((me // bit) % 2 + (k // bit) % 2) % 2 * bit
        bit *= 2
    return result


def wanted_slots(counts, table, pool_rows):
    prompts, page_most = table.shape[1:]
    rows = lax.broadcasted_iota(jnp.int32, (8, 128), 0)
    lanes = lax.broadcasted_iota(jnp.int32, (8, 128), 1)
    carry = (jnp.zeros((8, 128), jnp.int32), jnp.zeros((8, 128), jnp.int32))
    for prompt in range(prompts):
        length = counts[0, prompt]

        def place(j, carry, prompt=prompt, length=length):
            listed, ranks = carry
            page = table[0, prompt, j]
            owner = jnp.where(j < length, page // pool_rows, -1)
            hit = rows == owner
            code = (page - owner * pool_rows) * 2 + prompt
            listed = jnp.where(hit & (ranks == lanes), code, listed)
            return listed, jnp.where(hit, ranks + 1, ranks)

        carry = lax.fori_loop(0, page_most, place, carry)
    return carry[0]


def nt_dot(a, b):
    return lax.dot_general(a, b, (((1,), (1,)), ((), ())), preferred_element_type=jnp.float32)


def attend_kernel(
    dims,
    counts_hbm,
    table_hbm,
    scale_hbm,
    fill_hbm,
    queries_hbm,
    cache_hbm,
    fresh_hbm,
    pool_hbm,
    out_ref,
    counts_ref,
    table_ref,
    scale_raw,
    scale_wide,
    scale_ref,
    fill_ref,
    queries_ref,
    cache_ref,
    fresh_ref,
    request_ref,
    raw,
    keys,
    values,
    asked,
    asked_smem,
    query_slots,
    query_now,
    scores,
    sums,
    part_out,
    part_in,
    stat_out,
    stat_in,
    local_sum,
    local_stat,
    turned,
    load_sem,
    smem_sem,
    ask_send,
    ask_recv,
    query_send,
    query_recv,
    part_send,
    part_recv,
    stat_send,
    stat_recv,
):
    count, capacity, factor = dims
    pages = raw.shape[0]
    me = lax.axis_index("pre")
    partners = [partner_of(me, k, count) for k in range(count)]

    barrier = pltpu.get_barrier_semaphore()
    for k in range(1, count):
        pl.semaphore_signal(barrier, inc=1, device_id={"pre": partners[k]}, device_id_type=MESH)
    pairs = (
        (queries_hbm, queries_ref),
        (table_hbm, table_ref),
        (counts_hbm, counts_ref),
        (fresh_hbm, fresh_ref),
        (cache_hbm, cache_ref),
        (fill_hbm, fill_ref),
        (scale_hbm, scale_raw),
        (pool_hbm, raw),
    )
    loads = [pltpu.make_async_copy(a, b, load_sem.at[i]) for i, (a, b) in enumerate(pairs)]
    for load in loads:
        load.start()
    load_queries, load_table, load_counts, load_fresh, load_cache, load_fill, load_scale, load_pool = loads
    load_queries.wait()
    for prompt in range(2):
        for step in range(2):
            block = queries_ref[step, prompt * 16 : prompt * 16 + 16].astype(jnp.float32)
            for c in range(2):
                rows = block[:, c * 8 : c * 8 + 8, :].reshape(128, 128)
                query_slots[0, c, prompt, step * 128 : step * 128 + 128, :] = rows.astype(
                    jnp.bfloat16
                )
    pl.semaphore_wait(barrier, count - 1)

    def ask_copy(k, target):
        return pltpu.make_async_remote_copy(
            src_ref=request_ref.at[target],
            dst_ref=asked.at[k],
            send_sem=ask_send.at[k],
            recv_sem=ask_recv.at[k],
            device_id={"pre": target},
            device_id_type=MESH,
        )

    def query_copy(k, c, target):
        return pltpu.make_async_remote_copy(
            src_ref=query_slots.at[0, c],
            dst_ref=query_slots.at[k, c],
            send_sem=query_send.at[k, c],
            recv_sem=query_recv.at[k, c],
            device_id={"pre": target},
            device_id_type=MESH,
        )

    def part_copy(k, c, target):
        return pltpu.make_async_remote_copy(
            src_ref=part_out.at[k, c],
            dst_ref=part_in.at[k, c],
            send_sem=part_send.at[k, c],
            recv_sem=part_recv.at[k, c],
            device_id={"pre": target},
            device_id_type=MESH,
        )

    def stat_copy(k, c, target):
        return pltpu.make_async_remote_copy(
            src_ref=stat_out.at[k, c],
            dst_ref=stat_in.at[k, c],
            send_sem=stat_send.at[k, c],
            recv_sem=stat_recv.at[k, c],
            device_id={"pre": target},
            device_id_type=MESH,
        )

    for c in range(2):
        for k in range(1, count):
            query_copy(k, c, partners[k]).start()
    load_table.wait()
    load_counts.wait()
    listed = wanted_slots(counts_ref, table_ref, pages)
    for owner in range(count):
        request_ref[owner] = listed[owner : owner + 1]
    for k in range(1, count):
        ask_copy(k, partners[k]).start()
    own_ask = pltpu.make_async_copy(request_ref.at[me], asked_smem.at[0], smem_sem.at[0])
    own_ask.start()
    load_scale.wait()
    scale_wide[...] = scale_raw[...].astype(jnp.float32)
    widen = pltpu.make_async_copy(scale_wide, scale_ref, load_sem.at[6])
    widen.start()
    load_fresh.wait()
    load_cache.wait()
    load_fill.wait()

    to_row = lax.broadcasted_iota(jnp.int32, (256, 256), 0)
    from_row = lax.broadcasted_iota(jnp.int32, (256, 256), 1)
    order = jnp.where(from_row == (to_row % 64) * 4 + to_row // 64, 1.0, 0.0).astype(jnp.bfloat16)

    def sort_rows(block):
        return jnp.dot(order, block, preferred_element_type=jnp.float32)

    fresh_block = jnp.concatenate(
        [
            fresh_ref[step * 128 + prompt * 64 : step * 128 + prompt * 64 + 64, :]
            for prompt in range(2)
            for step in range(2)
        ],
        axis=0,
    )
    fresh_rows = sort_rows(fresh_block)
    key_at = lax.broadcasted_iota(jnp.int32, (128, 256), 0)
    query_at = lax.broadcasted_iota(jnp.int32, (128, 256), 1)
    query_sample = (query_at // 8) % 16
    is_cache = key_at < 64
    is_fresh = (key_at >= 64) & (key_at < 96)
    fresh_ok = is_fresh & (key_at % 16 == query_sample) & ((key_at - 64) // 16 <= query_at // 128)
    cache_same = is_cache & (key_at // 4 == query_sample)
    for prompt in range(2):
        cache_rows = sort_rows(cache_ref[prompt * 256 : prompt * 256 + 256, :])
        filled = jnp.zeros((128, 256), jnp.int32)
        for sample in range(16):
            filled = jnp.where(query_sample == sample, fill_ref[prompt * 16 + sample], filled)
        present = (cache_same & (key_at % 4 < filled)) | fresh_ok
        for c in range(2):

            def pick(kind):
                at = (c * 2 + kind) * 64
                return jnp.concatenate(
                    [
                        cache_rows[at : at + 64],
                        fresh_rows[at + prompt * 32 : at + prompt * 32 + 32],
                        jnp.zeros((32, 128), jnp.float32),
                    ],
                    axis=0,
                )

            part = nt_dot(pick(0).astype(jnp.bfloat16), query_slots[0, c, prompt]) * factor
            part = jnp.where(present, part, LOW)
            peak = jnp.max(part, axis=0, keepdims=True)
            grown = jnp.exp(part - peak)
            local_stat[c, prompt, 0:1, :] = peak
            local_stat[c, prompt, 1:2, :] = jnp.sum(grown, axis=0, keepdims=True)
            local_sum[c, prompt] = jnp.dot(
                pick(1).T.astype(jnp.bfloat16),
                grown.astype(jnp.bfloat16),
                preferred_element_type=jnp.float32,
            )

    load_pool.wait()

    def sort_page(page, carry):
        halves = [sort_rows(raw[page, h * 256 : h * 256 + 256, :]) for h in range(2)]
        for c in range(2):
            at = c * 128
            keys[page, c] = jnp.concatenate([x[at : at + 64] for x in halves], axis=0).astype(
                jnp.bfloat16
            )
            values[page, c] = jnp.concatenate(
                [x[at + 64 : at + 128] for x in halves], axis=0
            ).T.astype(jnp.bfloat16)
        return carry

    lax.fori_loop(0, pages, sort_page, 0)
    own_ask.wait()
    widen.wait()

    def serve(index, carry):
        c, k = index // count, index % count
        target = partner_of(me, k, count)

        @pl.when((c == 0) & (k > 0))
        def _():
            ask_copy(k, target).wait_recv()
            to_smem = pltpu.make_async_copy(asked.at[k], asked_smem.at[k], smem_sem.at[k])
            to_smem.start()
            to_smem.wait()

        @pl.when(k > 0)
        def _():
            query_copy(k, c, target).wait_recv()

        query_now[...] = query_slots[k, c]
        codes = [asked_smem[k, 0, j] for j in range(capacity)]
        slots = [code // 2 for code in codes]
        prompts = [code % 2 for code in codes]
        peaks = [jnp.full((1, 256), LOW, jnp.float32) for _ in range(2)]
        for j in range(capacity):
            key_scale = scale_ref[c, 0, slots[j]] * factor
            part = nt_dot(keys[slots[j], c], query_now[prompts[j]]) * key_scale
            scores[j] = part
            peak = jnp.max(part, axis=0, keepdims=True)
            for p in range(2):
                peaks[p] = jnp.maximum(peaks[p], jnp.where(prompts[j] == p, peak, LOW))
        totals = [jnp.zeros((1, 256), jnp.float32) for _ in range(2)]
        sums[...] = jnp.zeros_like(sums)
        for j in range(capacity):
            peak = jnp.where(prompts[j] == 0, peaks[0], peaks[1])
            grown = jnp.exp(scores[j] - peak)
            total = jnp.sum(grown, axis=0, keepdims=True)
            mixed = jnp.dot(
                values[slots[j], c],
                grown.astype(jnp.bfloat16),
                preferred_element_type=jnp.float32,
            )
            value_scale = scale_ref[c, 1, slots[j]]
            for p in range(2):
                totals[p] = totals[p] + jnp.where(prompts[j] == p, total, 0.0)
                sums[p] = sums[p] + mixed * jnp.where(prompts[j] == p, value_scale, 0.0)
        for p in range(2):
            mixed = sums[p]
            largest = jnp.max(jnp.abs(mixed), axis=0, keepdims=True)
            coded = jnp.round(mixed * (FULL / jnp.maximum(largest, 1e-30)))
            part_out[k, c, p] = coded.astype(jnp.int32).astype(jnp.int16)
            stat_out[k, c, p * 4 : p * 4 + 1, :] = peaks[p]
            stat_out[k, c, p * 4 + 1 : p * 4 + 2, :] = totals[p]
            stat_out[k, c, p * 4 + 2 : p * 4 + 3, :] = largest * (1.0 / FULL)
            stat_out[k, c, p * 4 + 3 : p * 4 + 4, :] = jnp.zeros((1, 256), jnp.float32)

        @pl.when(k > 0)
        def _():
            stat_copy(k, c, target).start()
            part_copy(k, c, target).start()

        return carry

    lax.fori_loop(0, 2 * count, serve, 0)

    for c in range(2):
        for k in range(1, count):
            stat_copy(k, c, partners[k]).wait_recv()
            part_copy(k, c, partners[k]).wait_recv()
        for p in range(2):
            stats = [stat_out[0, c]] + [stat_in[k, c] for k in range(1, count)]
            parts = [part_out[0, c, p]] + [part_in[k, c, p] for k in range(1, count)]
            local_peak = local_stat[c, p, 0:1, :]
            peak = local_peak
            for stat in stats:
                peak = jnp.maximum(peak, stat[p * 4 : p * 4 + 1])
            share = jnp.exp(local_peak - peak)
            total = share * local_stat[c, p, 1:2, :]
            mixed = local_sum[c, p] * share
            for stat, part in zip(stats, parts):
                share = jnp.exp(stat[p * 4 : p * 4 + 1] - peak)
                total = total + share * stat[p * 4 + 1 : p * 4 + 2]
                weight = share * stat[p * 4 + 2 : p * 4 + 3]
                mixed = mixed + part.astype(jnp.int32).astype(jnp.float32) * weight
            turned[p, c] = (mixed / total).T.reshape(2, 16, 8, 128)
    for p in range(2):
        both = jnp.concatenate([turned[p, 0], turned[p, 1]], axis=2)
        out_ref[:, p * 16 : p * 16 + 16] = both.astype(jnp.bfloat16)

    for k in range(1, count):
        ask_copy(k, partners[k]).wait_send()
        for c in range(2):
            query_copy(k, c, partners[k]).wait_send()
            stat_copy(k, c, partners[k]).wait_send()
            part_copy(k, c, partners[k]).wait_send()


def move_queries(
    page_pool, page_scales, queries, new_entries, token_cache, cache_fill, page_counts, page_table
):
    count = lax.axis_size("pre")
    pool_rows = page_pool.shape[0]
    capacity = pool_rows // count
    width = queries.shape[-1]
    vmem = pl.BlockSpec(memory_space=pltpu.VMEM)
    hbm = pl.BlockSpec(memory_space=pltpu.HBM)
    dma = pltpu.SemaphoreType.DMA
    f32, bf16 = jnp.float32, jnp.bfloat16
    return pl.pallas_call(
        functools.partial(attend_kernel, (count, capacity, 1.0 / math.sqrt(width))),
        out_shape=jax.ShapeDtypeStruct(queries.shape, queries.dtype),
        in_specs=[hbm] * 8,
        out_specs=vmem,
        scratch_shapes=[
            pltpu.SMEM(page_counts.shape, jnp.int32),
            pltpu.SMEM(page_table.shape, jnp.int32),
            pltpu.VMEM((2, 2, pool_rows), bf16),
            pltpu.VMEM((2, 2, pool_rows), f32),
            pltpu.SMEM((2, 2, pool_rows), f32),
            pltpu.SMEM(cache_fill.shape, jnp.int32),
            pltpu.VMEM(queries.shape, bf16),
            pltpu.VMEM((512, 128), bf16),
            pltpu.VMEM((256, 128), bf16),
            pltpu.VMEM((count, 1, 128), jnp.int32),
            pltpu.VMEM((pool_rows, 512, 128), bf16),
            pltpu.VMEM((pool_rows, 2, 128, 128), bf16),
            pltpu.VMEM((pool_rows, 2, 128, 128), bf16),
            pltpu.VMEM((count, 1, 128), jnp.int32),
            pltpu.SMEM((count, 1, 128), jnp.int32),
            pltpu.VMEM((count, 2, 2, 256, 128), bf16),
            pltpu.VMEM((2, 256, 128), bf16),
            pltpu.VMEM((capacity, 128, 256), f32),
            pltpu.VMEM((2, 128, 256), f32),
            pltpu.VMEM((count, 2, 2, 128, 256), jnp.int16),
            pltpu.VMEM((count, 2, 2, 128, 256), jnp.int16),
            pltpu.VMEM((count, 2, 8, 256), f32),
            pltpu.VMEM((count, 2, 8, 256), f32),
            pltpu.VMEM((2, 2, 128, 256), f32),
            pltpu.VMEM((2, 2, 8, 256), f32),
            pltpu.VMEM((2, 2, 2, 16, 8, 128), f32),
            dma((8,)),
            dma((count,)),
            dma((count,)),
            dma((count,)),
            dma((count, 2)),
            dma((count, 2)),
            dma((count, 2)),
            dma((count, 2)),
            dma((count, 2)),
            dma((count, 2)),
        ],
        compiler_params=pltpu.CompilerParams(
            collective_id=0, has_side_effects=True, vmem_limit_bytes=62 * 1024 * 1024
        ),
    )(
        page_counts,
        page_table,
        page_scales.transpose(1, 2, 0),
        cache_fill,
        queries,
        token_cache.reshape(-1, width),
        new_entries.reshape(-1, width),
        page_pool.reshape(pool_rows, -1, width),
    )


def shards(
    page_pool, page_scales, queries, new_entries, token_cache, cache_fill, page_counts, page_table
):
    args = (
        page_pool, page_scales, queries, new_entries, token_cache, cache_fill, page_counts, page_table,
    )
    count = lax.axis_size("pre")
    capacity = page_pool.shape[0] // count
    if count in (2, 4, 8) and capacity * page_pool[0].size > 2 * queries.size:
        return move_queries(*args)
    return move_pages(*args)


def solution(mesh):
    in_specs = (
        P(("groups", "pre"), None, "dec", None, None),
        P(("groups", "pre"), "dec", None),
        P(None, ("groups", "pre"), "dec", None),
        P(None, ("groups", "pre"), "dec", None, None),
        P(("groups", "pre"), None, "dec", None, None),
        P(("groups", "pre")),
        P(("groups", "pre"), None),
        P(("groups", "pre"), None, None),
    )
    out_specs = P(None, ("groups", "pre"), "dec", None)
    return jax.shard_map(shards, mesh=mesh, in_specs=in_specs, out_specs=out_specs, check_vma=False)
```

```python
import functools
import math

import jax
import jax.numpy as jnp
from jax import lax
from jax.experimental import pallas as pl
from jax.experimental.pallas import tpu as pltpu
from jax.sharding import PartitionSpec as P


def local_scores(grouped, cache_keys, fresh_keys, cache_fill, factor):
    cache_len = cache_keys.shape[2]
    step_count = fresh_keys.shape[1]
    cache_scores = (
        jnp.einsum("pctsgd,psicd->pctsgi", grouped, cache_keys, preferred_element_type=jnp.float32)
        * factor
    )
    present = (
        jnp.arange(cache_len, dtype=jnp.int32)[None, None, None, None, None, :]
        < cache_fill[:, None, None, :, None, None]
    )
    cache_scores = jnp.where(present, cache_scores, -jnp.inf)
    fresh_scores = (
        jnp.einsum("pctsgd,puscd->pctsgu", grouped, fresh_keys, preferred_element_type=jnp.float32)
        * factor
    )
    earlier = (
        jnp.arange(step_count, dtype=jnp.int32)[:, None]
        >= jnp.arange(step_count, dtype=jnp.int32)[None, :]
    )
    fresh_scores = jnp.where(earlier[None, None, :, None, None, :], fresh_scores, -jnp.inf)
    return (cache_scores, fresh_scores)


def local_terms(row_peak, cache_scores, fresh_scores, cache_values, fresh_values):
    cache_exp = jnp.exp(cache_scores - row_peak[..., None])
    fresh_exp = jnp.exp(fresh_scores - row_peak[..., None])
    denominator = jnp.sum(cache_exp, axis=-1) + jnp.sum(fresh_exp, axis=-1)
    mixed = jnp.einsum(
        "pctsgi,psicd->pctsgd",
        cache_exp.astype(jnp.bfloat16),
        cache_values,
        preferred_element_type=jnp.float32,
    )
    mixed = mixed + jnp.einsum(
        "pctsgu,puscd->pctsgd",
        fresh_exp.astype(jnp.bfloat16),
        fresh_values,
        preferred_element_type=jnp.float32,
    )
    return (denominator, mixed)


def request_table(group_table, lengths, pool_rows, pre_count, capacity):
    prompts, page_most = group_table.shape
    is_live = lax.broadcasted_iota(jnp.int32, (prompts, page_most), 1) < lengths[:, None]
    flat_ids = jnp.where(is_live, group_table, 0).reshape(-1)
    flat_live = is_live.reshape(-1)
    owners = jnp.where(flat_live, flat_ids // pool_rows, -1)
    pool_slots = flat_ids % pool_rows
    owner_hit = (owners[:, None] == lax.broadcasted_iota(jnp.int32, (1, pre_count), 1)).astype(
        jnp.int32
    )
    before = jnp.cumsum(owner_hit, axis=0) - owner_hit
    owner_rank = jnp.sum(before * owner_hit, axis=1)
    rank_hit = (owner_rank[:, None] == lax.broadcasted_iota(jnp.int32, (1, capacity), 1)).astype(
        jnp.int32
    )
    wanted = owner_hit[:, :, None] * rank_hit[:, None, :]
    requests = jnp.sum(wanted * (pool_slots + 1)[:, None, None], axis=0) - 1
    return (requests, owners, owner_rank, flat_live)


def pick_pages(page_pool, page_scales, wanted):
    flat_rows = jnp.maximum(wanted, 0).reshape(-1)
    page_block = jnp.take(page_pool, flat_rows, axis=0).reshape(wanted.shape + page_pool.shape[1:])
    scale_block = jnp.take(page_scales, flat_rows, axis=0).reshape(
        wanted.shape + page_scales.shape[1:]
    )
    return (page_block, scale_block)


def move_pages(
    page_pool, page_scales, queries, new_entries, token_cache, cache_fill, page_counts, page_table
):
    pre_count = lax.axis_size("pre")
    pool_rows = page_pool.shape[0]
    capacity = max(1, pool_rows // pre_count)
    kv_count = page_pool.shape[2]
    step_count, row_count, head_count, head_width = queries.shape
    prompts = page_counts.shape[1]
    page_most = page_table.shape[2]
    samples = row_count // prompts
    cache_len = token_cache.shape[1]
    head_ratio = head_count // kv_count
    factor = 1.0 / math.sqrt(head_width)
    requests, owners, owner_rank, flat_live = request_table(
        page_table[0], page_counts[0], pool_rows, pre_count, capacity
    )
    incoming = lax.all_to_all(requests, "pre", split_axis=0, concat_axis=0, tiled=True)
    page_block, scale_block = pick_pages(page_pool, page_scales, incoming)
    arrived, arrived_scales = (
        lax.all_to_all(page_block, "pre", split_axis=0, concat_axis=0, tiled=True),
        lax.all_to_all(scale_block, "pre", split_axis=0, concat_axis=0, tiled=True),
    )
    places = owners * capacity + owner_rank
    places = jnp.where(flat_live, places, 0)
    arrived = arrived.reshape((-1,) + page_pool.shape[1:])
    arrived_scales = arrived_scales.reshape((-1,) + page_scales.shape[1:])
    grouped = queries.reshape(
        step_count, prompts, samples, kv_count, head_ratio, head_width
    ).transpose(1, 3, 0, 2, 4, 5)
    cache_all = token_cache.reshape(prompts, samples, cache_len, kv_count, 2, head_width)
    fresh_all = new_entries.reshape(
        step_count, prompts, samples, kv_count, 2, head_width
    ).transpose(1, 0, 2, 3, 4, 5)
    filled = cache_fill.reshape(prompts, samples)
    cache_values = cache_all[..., 1, :]
    fresh_values = fresh_all[..., 1, :]
    cache_scores, fresh_scores = local_scores(
        grouped, cache_all[..., 0, :], fresh_all[..., 0, :], filled, factor
    )
    page_spots = places.reshape(prompts, page_most)
    live_pages = flat_live.reshape(prompts, page_most)

    def prompt_block(inputs):
        page_spot, live_row, prompt_query, cache_part, fresh_part, cache_vals, fresh_vals = inputs
        chosen = jnp.take(arrived, page_spot, axis=0)
        chosen_scales = jnp.take(arrived_scales, page_spot, axis=0).astype(jnp.float32)
        key_scale = chosen_scales[:, :, 0].T[:, None, None, None, :, None]
        prefix_scores = (
            jnp.einsum(
                "ctsgd,jicd->ctsgji",
                prompt_query,
                chosen[:, :, :, 0, :],
                preferred_element_type=jnp.float32,
            )
            * factor
            * key_scale
        )
        prefix_scores = jnp.where(live_row[:, None], prefix_scores, -jnp.inf)
        row_peak = jnp.maximum(
            jnp.max(prefix_scores, axis=(-2, -1)),
            jnp.maximum(jnp.max(cache_part, axis=-1), jnp.max(fresh_part, axis=-1)),
        )
        denominator, mixed = local_terms(
            row_peak[None], cache_part[None], fresh_part[None], cache_vals[None], fresh_vals[None]
        )
        prefix_exp = jnp.exp(prefix_scores - row_peak[..., None, None])
        denominator = denominator[0] + jnp.sum(prefix_exp, axis=(-2, -1))
        value_scale = chosen_scales[:, :, 1].T[:, None, None, None, :, None]
        per_page = jnp.einsum(
            "ctsgji,jicd->ctsgjd",
            prefix_exp.astype(jnp.bfloat16),
            chosen[:, :, :, 1, :],
            preferred_element_type=jnp.float32,
        )
        mixed = mixed[0] + jnp.sum(per_page * value_scale, axis=-2)
        return (mixed / denominator[..., None]).astype(jnp.bfloat16)

    result = lax.map(
        prompt_block,
        (page_spots, live_pages, grouped, cache_scores, fresh_scores, cache_values, fresh_values),
    )
    return result.transpose(2, 0, 3, 1, 4, 5).reshape(step_count, row_count, head_count, head_width)


MESH = pl.DeviceIdType.MESH
LOW = -1e30
FULL = 32000.0


def wanted_slots(counts, table, pool_rows):
    prompts, page_most = table.shape[1:]
    rows = lax.broadcasted_iota(jnp.int32, (8, 128), 0)
    lanes = lax.broadcasted_iota(jnp.int32, (8, 128), 1)
    carry = (jnp.zeros((8, 128), jnp.int32), jnp.zeros((8, 128), jnp.int32))
    for prompt in range(prompts):
        length = counts[0, prompt]

        def place(j, carry, prompt=prompt, length=length):
            listed, ranks = carry
            page = table[0, prompt, j]
            owner = jnp.where(j < length, page // pool_rows, -1)
            hit = rows == owner
            code = (page - owner * pool_rows) * 2 + prompt
            listed = jnp.where(hit & (ranks == lanes), code, listed)
            return listed, jnp.where(hit, ranks + 1, ranks)

        carry = lax.fori_loop(0, page_most, place, carry)
    return carry[0]


def nt_dot(a, b):
    return lax.dot_general(a, b, (((1,), (1,)), ((), ())), preferred_element_type=jnp.float32)


def attend_kernel(
    dims,
    counts_hbm,
    table_hbm,
    scale_hbm,
    fill_hbm,
    queries_hbm,
    cache_hbm,
    fresh_hbm,
    pool_hbm,
    out_ref,
    counts_ref,
    table_ref,
    scale_raw,
    scale_wide,
    scale_ref,
    fill_ref,
    queries_ref,
    cache_ref,
    fresh_ref,
    request_ref,
    raw,
    keys,
    values,
    asked,
    asked_smem,
    query_slots,
    query_now,
    scores,
    sums,
    sum_stat,
    part_out,
    part_in,
    stat_out,
    stat_in,
    local_sum,
    local_stat,
    turned,
    load_sem,
    smem_sem,
    ask_send,
    ask_recv,
    query_send,
    query_recv,
    part_send,
    part_recv,
    stat_send,
    stat_recv,
):
    count, capacity, factor = dims
    pages = raw.shape[0]
    me = lax.axis_index("pre")
    others = [lax.rem(me + k, count) for k in range(1, count)]

    barrier = pltpu.get_barrier_semaphore()
    for other in others:
        pl.semaphore_signal(barrier, inc=1, device_id={"pre": other}, device_id_type=MESH)
    pairs = (
        (queries_hbm, queries_ref),
        (table_hbm, table_ref),
        (counts_hbm, counts_ref),
        (fresh_hbm, fresh_ref),
        (cache_hbm, cache_ref),
        (fill_hbm, fill_ref),
        (scale_hbm, scale_raw),
        (pool_hbm, raw),
    )
    loads = [pltpu.make_async_copy(a, b, load_sem.at[i]) for i, (a, b) in enumerate(pairs)]
    for load in loads:
        load.start()
    load_queries, load_table, load_counts, load_fresh, load_cache, load_fill, load_scale, load_pool = loads
    load_queries.wait()
    for prompt in range(2):
        for step in range(2):
            block = queries_ref[step, prompt * 16 : prompt * 16 + 16].astype(jnp.float32)
            for c in range(2):
                rows = block[:, c * 8 : c * 8 + 8, :].reshape(128, 128)
                query_slots[me, c, prompt, step * 128 : step * 128 + 128, :] = rows.astype(
                    jnp.bfloat16
                )
    pl.semaphore_wait(barrier, count - 1)

    def ask_copy(source, target):
        return pltpu.make_async_remote_copy(
            src_ref=request_ref.at[target],
            dst_ref=asked.at[source],
            send_sem=ask_send.at[target],
            recv_sem=ask_recv.at[source],
            device_id={"pre": target},
            device_id_type=MESH,
        )

    def query_copy(group, c, way):
        return pltpu.make_async_remote_copy(
            src_ref=query_slots.at[group, c],
            dst_ref=query_slots.at[group, c],
            send_sem=query_send.at[group, c, way],
            recv_sem=query_recv.at[group, c],
            device_id={"pre": me + 1 - 2 * way},
            device_id_type=MESH,
        )

    def part_copy(group, c, way):
        return pltpu.make_async_remote_copy(
            src_ref=part_out.at[group, c],
            dst_ref=part_in.at[group + count * way, c],
            send_sem=part_send.at[group, c],
            recv_sem=part_recv.at[group + count * way, c],
            device_id={"pre": me + 1 - 2 * way},
            device_id_type=MESH,
        )

    def stat_copy(group, c, way):
        return pltpu.make_async_remote_copy(
            src_ref=stat_out.at[group, c],
            dst_ref=stat_in.at[group + count * way, c],
            send_sem=stat_send.at[group, c],
            recv_sem=stat_recv.at[group + count * way, c],
            device_id={"pre": me + 1 - 2 * way},
            device_id_type=MESH,
        )

    def has_next(way):
        return me < count - 1 if way == 0 else me > 0

    def send_queries(c):
        for way in range(2):

            @pl.when(has_next(way))
            def _(way=way):
                query_copy(me, c, way).start()

    def take_queries(c, distance):
        for way in range(2):
            group = me - distance if way == 0 else me + distance

            @pl.when((group >= 0) & (group < count))
            def _(way=way, group=group):
                query_copy(group, c, way).wait_recv()

                @pl.when(has_next(way))
                def _():
                    query_copy(group, c, way).start()

    send_queries(0)
    load_table.wait()
    load_counts.wait()
    listed = wanted_slots(counts_ref, table_ref, pages)
    for owner in range(count):
        request_ref[owner] = listed[owner : owner + 1]
    for other in others:
        ask_copy(me, other).start()
    own_ask = pltpu.make_async_copy(request_ref.at[me], asked_smem.at[me], smem_sem.at[me])
    own_ask.start()
    load_scale.wait()
    scale_wide[...] = scale_raw[...].astype(jnp.float32)
    widen = pltpu.make_async_copy(scale_wide, scale_ref, load_sem.at[6])
    widen.start()
    load_fresh.wait()
    load_cache.wait()
    load_fill.wait()

    to_row = lax.broadcasted_iota(jnp.int32, (256, 256), 0)
    from_row = lax.broadcasted_iota(jnp.int32, (256, 256), 1)
    order = jnp.where(from_row == (to_row % 64) * 4 + to_row // 64, 1.0, 0.0).astype(jnp.bfloat16)

    def sort_rows(block):
        return jnp.dot(order, block, preferred_element_type=jnp.float32)

    fresh_block = jnp.concatenate(
        [
            fresh_ref[step * 128 + prompt * 64 : step * 128 + prompt * 64 + 64, :]
            for prompt in range(2)
            for step in range(2)
        ],
        axis=0,
    )
    fresh_rows = sort_rows(fresh_block)
    key_at = lax.broadcasted_iota(jnp.int32, (128, 256), 0)
    query_at = lax.broadcasted_iota(jnp.int32, (128, 256), 1)
    query_sample = (query_at // 8) % 16
    is_cache = key_at < 64
    is_fresh = (key_at >= 64) & (key_at < 96)
    fresh_ok = is_fresh & (key_at % 16 == query_sample) & ((key_at - 64) // 16 <= query_at // 128)
    cache_same = is_cache & (key_at // 4 == query_sample)
    for prompt in range(2):
        cache_rows = sort_rows(cache_ref[prompt * 256 : prompt * 256 + 256, :])
        filled = jnp.zeros((128, 256), jnp.int32)
        for sample in range(16):
            filled = jnp.where(query_sample == sample, fill_ref[prompt * 16 + sample], filled)
        present = (cache_same & (key_at % 4 < filled)) | fresh_ok
        for c in range(2):

            def pick(kind):
                at = (c * 2 + kind) * 64
                return jnp.concatenate(
                    [
                        cache_rows[at : at + 64],
                        fresh_rows[at + prompt * 32 : at + prompt * 32 + 32],
                        jnp.zeros((32, 128), jnp.float32),
                    ],
                    axis=0,
                )

            part = nt_dot(pick(0).astype(jnp.bfloat16), query_slots[me, c, prompt]) * factor
            part = jnp.where(present, part, LOW)
            peak = jnp.max(part, axis=0, keepdims=True)
            grown = jnp.exp(part - peak)
            local_stat[c, prompt, 0:1, :] = peak
            local_stat[c, prompt, 1:2, :] = jnp.sum(grown, axis=0, keepdims=True)
            local_sum[c, prompt] = jnp.dot(
                pick(1).T.astype(jnp.bfloat16),
                grown.astype(jnp.bfloat16),
                preferred_element_type=jnp.float32,
            )

    load_pool.wait()

    def sort_pages(block, carry):
        for i in range(4):
            page = block * 4 + i
            sides = jnp.concatenate([raw[page, :256, :], raw[page, 256:, :]], axis=1)
            rows = sort_rows(sides)
            for c in range(2):
                at = c * 128
                keys[page, c, :64] = rows[at : at + 64, :128].astype(jnp.bfloat16)
                keys[page, c, 64:] = rows[at : at + 64, 128:].astype(jnp.bfloat16)
                held = rows[at + 64 : at + 128]
                values[page, c] = jnp.concatenate(
                    [held[:, :128], held[:, 128:]], axis=0
                ).T.astype(jnp.bfloat16)
        return carry

    blocks = pages // 4
    for turn in range(count):
        lax.fori_loop(blocks * turn // count, blocks * (turn + 1) // count, sort_pages, 0)
        if turn < count - 1:
            take_queries(0, turn + 1)
        if turn == count // 2 - 1:
            send_queries(1)
    own_ask.wait()
    widen.wait()
    for other in others:
        ask_copy(other, me).wait_recv()
        to_smem = pltpu.make_async_copy(asked.at[other], asked_smem.at[other], smem_sem.at[other])
        to_smem.start()
        to_smem.wait()

    def code_and_send(group, c, way):
        for p in range(2):
            mixed = sums[group, c, p]
            largest = jnp.max(jnp.abs(mixed), axis=0, keepdims=True)
            coded = jnp.round(mixed * (FULL / jnp.maximum(largest, 1e-30)))
            part_out[group, c, p] = coded.astype(jnp.int32).astype(jnp.int16)
            stat_out[group, c, p * 4 : p * 4 + 2, :] = sum_stat[group, c, p * 4 : p * 4 + 2, :]
            stat_out[group, c, p * 4 + 2 : p * 4 + 3, :] = largest * (1.0 / FULL)
            stat_out[group, c, p * 4 + 3 : p * 4 + 4, :] = jnp.zeros((1, 256), jnp.float32)
        stat_copy(group, c, way).start()
        part_copy(group, c, way).start()

    def add_incoming(group, c, way):
        stat_copy(group, c, way).wait_recv()
        part_copy(group, c, way).wait_recv()
        slot = group + count * way
        for p in range(2):
            at = p * 4
            there = stat_in[slot, c, at : at + 1, :]
            here = sum_stat[group, c, at : at + 1, :]
            peak = jnp.maximum(here, there)
            keep, add = jnp.exp(here - peak), jnp.exp(there - peak)
            sum_stat[group, c, at : at + 1, :] = peak
            sum_stat[group, c, at + 1 : at + 2, :] = (
                sum_stat[group, c, at + 1 : at + 2, :] * keep
                + stat_in[slot, c, at + 1 : at + 2, :] * add
            )
            part = part_in[slot, c, p].astype(jnp.int32).astype(jnp.float32)
            sums[group, c, p] = sums[group, c, p] * keep + part * (
                add * stat_in[slot, c, at + 2 : at + 3, :]
            )

    def attend(group, c):
        query_now[...] = query_slots[group, c]
        codes = [asked_smem[group, 0, j] for j in range(capacity)]
        slots = [code // 2 for code in codes]
        prompts = [code % 2 for code in codes]
        peaks = [jnp.full((1, 256), LOW, jnp.float32) for _ in range(2)]
        for j in range(capacity):
            key_scale = scale_ref[c, 0, slots[j]] * factor
            part = nt_dot(keys[slots[j], c], query_now[prompts[j]]) * key_scale
            scores[j] = part
            peak = jnp.max(part, axis=0, keepdims=True)
            for p in range(2):
                peaks[p] = jnp.maximum(peaks[p], jnp.where(prompts[j] == p, peak, LOW))
        totals = [jnp.zeros((1, 256), jnp.float32) for _ in range(2)]
        sums[group, c] = jnp.zeros((2, 128, 256), jnp.float32)
        for j in range(capacity):
            peak = jnp.where(prompts[j] == 0, peaks[0], peaks[1])
            grown = jnp.exp(scores[j] - peak)
            total = jnp.sum(grown, axis=0, keepdims=True)
            mixed = jnp.dot(
                values[slots[j], c],
                grown.astype(jnp.bfloat16),
                preferred_element_type=jnp.float32,
            )
            value_scale = scale_ref[c, 1, slots[j]]
            for p in range(2):
                totals[p] = totals[p] + jnp.where(prompts[j] == p, total, 0.0)
                sums[group, c, p] = sums[group, c, p] + mixed * jnp.where(prompts[j] == p, value_scale, 0.0)
        for p in range(2):
            sum_stat[group, c, p * 4 : p * 4 + 1, :] = peaks[p]
            sum_stat[group, c, p * 4 + 1 : p * 4 + 2, :] = totals[p]

    def serve(index, c):
        way = index % 2
        group = me + (1 - 2 * way) * (count - 1 - index // 2)

        @pl.when((group >= 0) & (group < count) & (index < 2 * count - 1))
        def _():
            attend(group, c)

            @pl.when((group != me) & (me == way * (count - 1)))
            def _():
                code_and_send(group, c, way)

        return c

    def pass_on(c, passed):
        for distance in range(count - 1 - passed, 0, -1):
            for way in range(2):
                group = me + (1 - 2 * way) * distance
                behind = me if way == 0 else count - 1 - me

                @pl.when((group >= 0) & (group < count) & (behind == passed))
                def _(way=way, group=group):
                    add_incoming(group, c, way)
                    code_and_send(group, c, way)

    def finish(c):
        for way in range(2):

            @pl.when(has_next(1 - way))
            def _(way=way):
                add_incoming(me, c, way)

        for p in range(2):
            at = p * 4
            here = sum_stat[me, c, at : at + 1, :]
            local_peak = local_stat[c, p, 0:1, :]
            peak = jnp.maximum(here, local_peak)
            keep, add = jnp.exp(here - peak), jnp.exp(local_peak - peak)
            total = keep * sum_stat[me, c, at + 1 : at + 2, :] + add * local_stat[c, p, 1:2, :]
            mixed = sums[me, c, p] * (keep / total) + local_sum[c, p] * (add / total)
            turned[p, c] = mixed.T.reshape(2, 16, 8, 128)

    lax.fori_loop(0, 2 * count - 1, serve, 0)
    for distance in range(1, count):
        take_queries(1, distance)
        if distance == 1 and count > 2:
            pass_on(0, 1)
    lax.fori_loop(0, 2 * count - 1, serve, 1)
    for passed in range(2, count - 1):
        pass_on(0, passed)
    finish(0)
    for passed in range(1, count - 1):
        pass_on(1, passed)
    finish(1)
    for p in range(2):
        both = jnp.concatenate([turned[p, 0], turned[p, 1]], axis=2)
        out_ref[:, p * 16 : p * 16 + 16] = both.astype(jnp.bfloat16)

    for other in others:
        ask_copy(me, other).wait_send()
    for c in range(2):
        for way in range(2):
            for distance in range(count):
                group = me - distance if way == 0 else me + distance

                @pl.when((group >= 0) & (group < count) & has_next(way))
                def _(way=way, group=group, c=c):
                    query_copy(group, c, way).wait_send()

                target = me + distance if way == 0 else me - distance
                if distance > 0:

                    @pl.when((target >= 0) & (target < count))
                    def _(way=way, target=target, c=c):
                        stat_copy(target, c, way).wait_send()
                        part_copy(target, c, way).wait_send()


def move_queries(
    page_pool, page_scales, queries, new_entries, token_cache, cache_fill, page_counts, page_table
):
    count = lax.axis_size("pre")
    pool_rows = page_pool.shape[0]
    capacity = pool_rows // count
    width = queries.shape[-1]
    vmem = pl.BlockSpec(memory_space=pltpu.VMEM)
    hbm = pl.BlockSpec(memory_space=pltpu.HBM)
    dma = pltpu.SemaphoreType.DMA
    f32, bf16 = jnp.float32, jnp.bfloat16
    return pl.pallas_call(
        functools.partial(attend_kernel, (count, capacity, 1.0 / math.sqrt(width))),
        out_shape=jax.ShapeDtypeStruct(queries.shape, queries.dtype),
        in_specs=[hbm] * 8,
        out_specs=vmem,
        scratch_shapes=[
            pltpu.SMEM(page_counts.shape, jnp.int32),
            pltpu.SMEM(page_table.shape, jnp.int32),
            pltpu.VMEM((2, 2, pool_rows), bf16),
            pltpu.VMEM((2, 2, pool_rows), f32),
            pltpu.SMEM((2, 2, pool_rows), f32),
            pltpu.SMEM(cache_fill.shape, jnp.int32),
            pltpu.VMEM(queries.shape, bf16),
            pltpu.VMEM((512, 128), bf16),
            pltpu.VMEM((256, 128), bf16),
            pltpu.VMEM((count, 1, 128), jnp.int32),
            pltpu.VMEM((pool_rows, 512, 128), bf16),
            pltpu.VMEM((pool_rows, 2, 128, 128), bf16),
            pltpu.VMEM((pool_rows, 2, 128, 128), bf16),
            pltpu.VMEM((count, 1, 128), jnp.int32),
            pltpu.SMEM((count, 1, 128), jnp.int32),
            pltpu.VMEM((count, 2, 2, 256, 128), bf16),
            pltpu.VMEM((2, 256, 128), bf16),
            pltpu.VMEM((capacity, 128, 256), f32),
            pltpu.VMEM((count, 2, 2, 128, 256), f32),
            pltpu.VMEM((count, 2, 8, 256), f32),
            pltpu.VMEM((count, 2, 2, 128, 256), jnp.int16),
            pltpu.VMEM((2 * count, 2, 2, 128, 256), jnp.int16),
            pltpu.VMEM((count, 2, 8, 256), f32),
            pltpu.VMEM((2 * count, 2, 8, 256), f32),
            pltpu.VMEM((2, 2, 128, 256), f32),
            pltpu.VMEM((2, 2, 8, 256), f32),
            pltpu.VMEM((2, 2, 2, 16, 8, 128), f32),
            dma((8,)),
            dma((count,)),
            dma((count,)),
            dma((count,)),
            dma((count, 2, 2)),
            dma((count, 2)),
            dma((count, 2)),
            dma((2 * count, 2)),
            dma((count, 2)),
            dma((2 * count, 2)),
        ],
        compiler_params=pltpu.CompilerParams(
            collective_id=0, has_side_effects=True, vmem_limit_bytes=62 * 1024 * 1024
        ),
    )(
        page_counts,
        page_table,
        page_scales.transpose(1, 2, 0),
        cache_fill,
        queries,
        token_cache.reshape(-1, width),
        new_entries.reshape(-1, width),
        page_pool.reshape(pool_rows, -1, width),
    )


def shards(
    page_pool, page_scales, queries, new_entries, token_cache, cache_fill, page_counts, page_table
):
    args = (
        page_pool, page_scales, queries, new_entries, token_cache, cache_fill, page_counts, page_table,
    )
    count = lax.axis_size("pre")
    capacity = page_pool.shape[0] // count
    if count in (2, 4, 8) and page_pool.shape[0] % (4 * count) == 0 and capacity * page_pool[0].size > 2 * queries.size:
        return move_queries(*args)
    return move_pages(*args)


def solution(mesh):
    in_specs = (
        P(("groups", "pre"), None, "dec", None, None),
        P(("groups", "pre"), "dec", None),
        P(None, ("groups", "pre"), "dec", None),
        P(None, ("groups", "pre"), "dec", None, None),
        P(("groups", "pre"), None, "dec", None, None),
        P(("groups", "pre")),
        P(("groups", "pre"), None),
        P(("groups", "pre"), None, None),
    )
    out_specs = P(None, ("groups", "pre"), "dec", None)
    return jax.shard_map(shards, mesh=mesh, in_specs=in_specs, out_specs=out_specs, check_vma=False)
```

```python
import functools
import math

import jax
import jax.numpy as jnp
from jax import lax
from jax.experimental import pallas as pl
from jax.experimental.pallas import tpu as pltpu
from jax.sharding import PartitionSpec as P


def local_scores(grouped, cache_keys, fresh_keys, cache_fill, factor):
    cache_len = cache_keys.shape[2]
    step_count = fresh_keys.shape[1]
    cache_scores = (
        jnp.einsum("pctsgd,psicd->pctsgi", grouped, cache_keys, preferred_element_type=jnp.float32)
        * factor
    )
    present = (
        jnp.arange(cache_len, dtype=jnp.int32)[None, None, None, None, None, :]
        < cache_fill[:, None, None, :, None, None]
    )
    cache_scores = jnp.where(present, cache_scores, -jnp.inf)
    fresh_scores = (
        jnp.einsum("pctsgd,puscd->pctsgu", grouped, fresh_keys, preferred_element_type=jnp.float32)
        * factor
    )
    earlier = (
        jnp.arange(step_count, dtype=jnp.int32)[:, None]
        >= jnp.arange(step_count, dtype=jnp.int32)[None, :]
    )
    fresh_scores = jnp.where(earlier[None, None, :, None, None, :], fresh_scores, -jnp.inf)
    return (cache_scores, fresh_scores)


def local_terms(row_peak, cache_scores, fresh_scores, cache_values, fresh_values):
    cache_exp = jnp.exp(cache_scores - row_peak[..., None])
    fresh_exp = jnp.exp(fresh_scores - row_peak[..., None])
    denominator = jnp.sum(cache_exp, axis=-1) + jnp.sum(fresh_exp, axis=-1)
    mixed = jnp.einsum(
        "pctsgi,psicd->pctsgd",
        cache_exp.astype(jnp.bfloat16),
        cache_values,
        preferred_element_type=jnp.float32,
    )
    mixed = mixed + jnp.einsum(
        "pctsgu,puscd->pctsgd",
        fresh_exp.astype(jnp.bfloat16),
        fresh_values,
        preferred_element_type=jnp.float32,
    )
    return (denominator, mixed)


def request_table(group_table, lengths, pool_rows, pre_count, capacity):
    prompts, page_most = group_table.shape
    is_live = lax.broadcasted_iota(jnp.int32, (prompts, page_most), 1) < lengths[:, None]
    flat_ids = jnp.where(is_live, group_table, 0).reshape(-1)
    flat_live = is_live.reshape(-1)
    owners = jnp.where(flat_live, flat_ids // pool_rows, -1)
    pool_slots = flat_ids % pool_rows
    owner_hit = (owners[:, None] == lax.broadcasted_iota(jnp.int32, (1, pre_count), 1)).astype(
        jnp.int32
    )
    before = jnp.cumsum(owner_hit, axis=0) - owner_hit
    owner_rank = jnp.sum(before * owner_hit, axis=1)
    rank_hit = (owner_rank[:, None] == lax.broadcasted_iota(jnp.int32, (1, capacity), 1)).astype(
        jnp.int32
    )
    wanted = owner_hit[:, :, None] * rank_hit[:, None, :]
    requests = jnp.sum(wanted * (pool_slots + 1)[:, None, None], axis=0) - 1
    return (requests, owners, owner_rank, flat_live)


def pick_pages(page_pool, page_scales, wanted):
    flat_rows = jnp.maximum(wanted, 0).reshape(-1)
    page_block = jnp.take(page_pool, flat_rows, axis=0).reshape(wanted.shape + page_pool.shape[1:])
    scale_block = jnp.take(page_scales, flat_rows, axis=0).reshape(
        wanted.shape + page_scales.shape[1:]
    )
    return (page_block, scale_block)


def move_pages(
    page_pool, page_scales, queries, new_entries, token_cache, cache_fill, page_counts, page_table
):
    pre_count = lax.axis_size("pre")
    pool_rows = page_pool.shape[0]
    capacity = max(1, pool_rows // pre_count)
    kv_count = page_pool.shape[2]
    step_count, row_count, head_count, head_width = queries.shape
    prompts = page_counts.shape[1]
    page_most = page_table.shape[2]
    samples = row_count // prompts
    cache_len = token_cache.shape[1]
    head_ratio = head_count // kv_count
    factor = 1.0 / math.sqrt(head_width)
    requests, owners, owner_rank, flat_live = request_table(
        page_table[0], page_counts[0], pool_rows, pre_count, capacity
    )
    incoming = lax.all_to_all(requests, "pre", split_axis=0, concat_axis=0, tiled=True)
    page_block, scale_block = pick_pages(page_pool, page_scales, incoming)
    arrived, arrived_scales = (
        lax.all_to_all(page_block, "pre", split_axis=0, concat_axis=0, tiled=True),
        lax.all_to_all(scale_block, "pre", split_axis=0, concat_axis=0, tiled=True),
    )
    places = owners * capacity + owner_rank
    places = jnp.where(flat_live, places, 0)
    arrived = arrived.reshape((-1,) + page_pool.shape[1:])
    arrived_scales = arrived_scales.reshape((-1,) + page_scales.shape[1:])
    grouped = queries.reshape(
        step_count, prompts, samples, kv_count, head_ratio, head_width
    ).transpose(1, 3, 0, 2, 4, 5)
    cache_all = token_cache.reshape(prompts, samples, cache_len, kv_count, 2, head_width)
    fresh_all = new_entries.reshape(
        step_count, prompts, samples, kv_count, 2, head_width
    ).transpose(1, 0, 2, 3, 4, 5)
    filled = cache_fill.reshape(prompts, samples)
    cache_values = cache_all[..., 1, :]
    fresh_values = fresh_all[..., 1, :]
    cache_scores, fresh_scores = local_scores(
        grouped, cache_all[..., 0, :], fresh_all[..., 0, :], filled, factor
    )
    page_spots = places.reshape(prompts, page_most)
    live_pages = flat_live.reshape(prompts, page_most)

    def prompt_block(inputs):
        page_spot, live_row, prompt_query, cache_part, fresh_part, cache_vals, fresh_vals = inputs
        chosen = jnp.take(arrived, page_spot, axis=0)
        chosen_scales = jnp.take(arrived_scales, page_spot, axis=0).astype(jnp.float32)
        key_scale = chosen_scales[:, :, 0].T[:, None, None, None, :, None]
        prefix_scores = (
            jnp.einsum(
                "ctsgd,jicd->ctsgji",
                prompt_query,
                chosen[:, :, :, 0, :],
                preferred_element_type=jnp.float32,
            )
            * factor
            * key_scale
        )
        prefix_scores = jnp.where(live_row[:, None], prefix_scores, -jnp.inf)
        row_peak = jnp.maximum(
            jnp.max(prefix_scores, axis=(-2, -1)),
            jnp.maximum(jnp.max(cache_part, axis=-1), jnp.max(fresh_part, axis=-1)),
        )
        denominator, mixed = local_terms(
            row_peak[None], cache_part[None], fresh_part[None], cache_vals[None], fresh_vals[None]
        )
        prefix_exp = jnp.exp(prefix_scores - row_peak[..., None, None])
        denominator = denominator[0] + jnp.sum(prefix_exp, axis=(-2, -1))
        value_scale = chosen_scales[:, :, 1].T[:, None, None, None, :, None]
        per_page = jnp.einsum(
            "ctsgji,jicd->ctsgjd",
            prefix_exp.astype(jnp.bfloat16),
            chosen[:, :, :, 1, :],
            preferred_element_type=jnp.float32,
        )
        mixed = mixed[0] + jnp.sum(per_page * value_scale, axis=-2)
        return (mixed / denominator[..., None]).astype(jnp.bfloat16)

    result = lax.map(
        prompt_block,
        (page_spots, live_pages, grouped, cache_scores, fresh_scores, cache_values, fresh_values),
    )
    return result.transpose(2, 0, 3, 1, 4, 5).reshape(step_count, row_count, head_count, head_width)


MESH = pl.DeviceIdType.MESH
LOW = -1e30
FULL = 32000.0


def wanted_slots(counts, table, pool_rows):
    prompts, page_most = table.shape[1:]
    rows = lax.broadcasted_iota(jnp.int32, (8, 128), 0)
    lanes = lax.broadcasted_iota(jnp.int32, (8, 128), 1)
    carry = (jnp.zeros((8, 128), jnp.int32), jnp.zeros((8, 128), jnp.int32))
    for prompt in range(prompts):
        length = counts[0, prompt]

        def place(j, carry, prompt=prompt, length=length):
            listed, ranks = carry
            page = table[0, prompt, j]
            owner = jnp.where(j < length, page // pool_rows, -1)
            hit = rows == owner
            code = (page - owner * pool_rows) * 2 + prompt
            listed = jnp.where(hit & (ranks == lanes), code, listed)
            return listed, jnp.where(hit, ranks + 1, ranks)

        carry = lax.fori_loop(0, page_most, place, carry)
    return carry[0]


def nt_dot(a, b):
    return lax.dot_general(a, b, (((1,), (1,)), ((), ())), preferred_element_type=jnp.float32)


def attend_kernel(
    dims,
    counts_hbm,
    table_hbm,
    scale_hbm,
    fill_hbm,
    queries_hbm,
    cache_hbm,
    fresh_hbm,
    pool_hbm,
    out_ref,
    counts_ref,
    table_ref,
    scale_raw,
    scale_wide,
    scale_ref,
    fill_ref,
    queries_ref,
    cache_ref,
    fresh_ref,
    request_ref,
    raw,
    keys,
    values,
    asked,
    asked_smem,
    query_slots,
    query_now,
    scores,
    sums,
    sum_stat,
    part_out,
    part_in,
    stat_out,
    stat_in,
    local_sum,
    local_stat,
    turned,
    load_sem,
    smem_sem,
    ask_send,
    ask_recv,
    query_send,
    query_recv,
    part_send,
    part_recv,
    stat_send,
    stat_recv,
):
    count, capacity, factor = dims
    pages = raw.shape[0]
    me = lax.axis_index("pre")
    others = [lax.rem(me + k, count) for k in range(1, count)]

    barrier = pltpu.get_barrier_semaphore()
    for other in others:
        pl.semaphore_signal(barrier, inc=1, device_id={"pre": other}, device_id_type=MESH)
    pairs = (
        (queries_hbm, queries_ref),
        (table_hbm, table_ref),
        (counts_hbm, counts_ref),
        (fresh_hbm, fresh_ref),
        (cache_hbm, cache_ref),
        (fill_hbm, fill_ref),
        (scale_hbm, scale_raw),
        (pool_hbm, raw),
    )
    loads = [pltpu.make_async_copy(a, b, load_sem.at[i]) for i, (a, b) in enumerate(pairs)]
    for load in loads:
        load.start()
    load_queries, load_table, load_counts, load_fresh, load_cache, load_fill, load_scale, load_pool = loads
    load_queries.wait()
    for prompt in range(2):
        for step in range(2):
            block = queries_ref[step, prompt * 16 : prompt * 16 + 16].astype(jnp.float32)
            for c in range(2):
                rows = block[:, c * 8 : c * 8 + 8, :].reshape(128, 128)
                query_slots[me, c, prompt, step * 128 : step * 128 + 128, :] = rows.astype(
                    jnp.bfloat16
                )
    pl.semaphore_wait(barrier, count - 1)

    def ask_copy(source, target):
        return pltpu.make_async_remote_copy(
            src_ref=request_ref.at[target],
            dst_ref=asked.at[source],
            send_sem=ask_send.at[target],
            recv_sem=ask_recv.at[source],
            device_id={"pre": target},
            device_id_type=MESH,
        )

    def query_copy(group, c, way):
        return pltpu.make_async_remote_copy(
            src_ref=query_slots.at[group, c],
            dst_ref=query_slots.at[group, c],
            send_sem=query_send.at[group, c, way],
            recv_sem=query_recv.at[group, c],
            device_id={"pre": me + 1 - 2 * way},
            device_id_type=MESH,
        )

    def part_copy(group, c, way):
        return pltpu.make_async_remote_copy(
            src_ref=part_out.at[group, c],
            dst_ref=part_in.at[group + count * way, c],
            send_sem=part_send.at[group, c],
            recv_sem=part_recv.at[group + count * way, c],
            device_id={"pre": me + 1 - 2 * way},
            device_id_type=MESH,
        )

    def stat_copy(group, c, way):
        return pltpu.make_async_remote_copy(
            src_ref=stat_out.at[group, c],
            dst_ref=stat_in.at[group + count * way, c],
            send_sem=stat_send.at[group, c],
            recv_sem=stat_recv.at[group + count * way, c],
            device_id={"pre": me + 1 - 2 * way},
            device_id_type=MESH,
        )

    def has_next(way):
        ahead = me + 1 - 2 * way
        return (ahead >= 0) & (ahead < count)

    def send_queries(c, way, when):
        @pl.when(when & has_next(way))
        def _():
            query_copy(me, c, way).start()

    def take_queries(group, c, way):
        query_copy(group, c, way).wait_recv()

        @pl.when(has_next(way))
        def _():
            query_copy(group, c, way).start()

    for way in range(2):
        send_queries(0, way, me >= 0)
    for way in range(2):
        send_queries(1, way, me == way * (count - 1))
    load_table.wait()
    load_counts.wait()
    listed = wanted_slots(counts_ref, table_ref, pages)
    for owner in range(count):
        request_ref[owner] = listed[owner : owner + 1]
    for other in others:
        ask_copy(me, other).start()
    own_ask = pltpu.make_async_copy(request_ref.at[me], asked_smem.at[me], smem_sem.at[me])
    own_ask.start()
    load_scale.wait()
    scale_wide[...] = scale_raw[...].astype(jnp.float32)
    widen = pltpu.make_async_copy(scale_wide, scale_ref, load_sem.at[6])
    widen.start()
    load_fresh.wait()
    load_cache.wait()
    load_fill.wait()

    to_row = lax.broadcasted_iota(jnp.int32, (256, 256), 0)
    from_row = lax.broadcasted_iota(jnp.int32, (256, 256), 1)
    order = jnp.where(from_row == (to_row % 64) * 4 + to_row // 64, 1.0, 0.0).astype(jnp.bfloat16)

    def sort_rows(block):
        return jnp.dot(order, block, preferred_element_type=jnp.float32)

    load_pool.wait()

    def sort_pages(block, carry):
        for i in range(4):
            page = block * 4 + i
            sides = jnp.concatenate([raw[page, :256, :], raw[page, 256:, :]], axis=1)
            rows = sort_rows(sides)
            for c in range(2):
                at = c * 128
                keys[page, c, :64] = rows[at : at + 64, :128].astype(jnp.bfloat16)
                keys[page, c, 64:] = rows[at : at + 64, 128:].astype(jnp.bfloat16)
                held = rows[at + 64 : at + 128]
                values[page, c] = jnp.concatenate(
                    [held[:, :128], held[:, 128:]], axis=0
                ).T.astype(jnp.bfloat16)
        return carry

    blocks = pages // 4
    def take_near(distance):
        for way in range(2):
            group = me - (1 - 2 * way) * distance

            @pl.when((group >= 0) & (group < count))
            def _(way=way, group=group):
                take_queries(group, 0, way)

    lax.fori_loop(0, blocks // 2, sort_pages, 0)
    take_near(1)
    lax.fori_loop(blocks // 2, blocks, sort_pages, 0)
    if count > 2:
        take_near(2)

    fresh_block = jnp.concatenate(
        [
            fresh_ref[step * 128 + prompt * 64 : step * 128 + prompt * 64 + 64, :]
            for prompt in range(2)
            for step in range(2)
        ],
        axis=0,
    )
    fresh_rows = sort_rows(fresh_block)
    key_at = lax.broadcasted_iota(jnp.int32, (128, 256), 0)
    query_at = lax.broadcasted_iota(jnp.int32, (128, 256), 1)
    query_sample = (query_at // 8) % 16
    is_cache = key_at < 64
    is_fresh = (key_at >= 64) & (key_at < 96)
    fresh_ok = is_fresh & (key_at % 16 == query_sample) & ((key_at - 64) // 16 <= query_at // 128)
    cache_same = is_cache & (key_at // 4 == query_sample)
    for prompt in range(2):
        cache_rows = sort_rows(cache_ref[prompt * 256 : prompt * 256 + 256, :])
        filled = jnp.zeros((128, 256), jnp.int32)
        for sample in range(16):
            filled = jnp.where(query_sample == sample, fill_ref[prompt * 16 + sample], filled)
        present = (cache_same & (key_at % 4 < filled)) | fresh_ok
        for c in range(2):

            def pick(kind):
                at = (c * 2 + kind) * 64
                return jnp.concatenate(
                    [
                        cache_rows[at : at + 64],
                        fresh_rows[at + prompt * 32 : at + prompt * 32 + 32],
                        jnp.zeros((32, 128), jnp.float32),
                    ],
                    axis=0,
                )

            part = nt_dot(pick(0).astype(jnp.bfloat16), query_slots[me, c, prompt]) * factor
            part = jnp.where(present, part, LOW)
            peak = jnp.max(part, axis=0, keepdims=True)
            grown = jnp.exp(part - peak)
            local_stat[c, prompt, 0:1, :] = peak
            local_stat[c, prompt, 1:2, :] = jnp.sum(grown, axis=0, keepdims=True)
            local_sum[c, prompt] = jnp.dot(
                pick(1).T.astype(jnp.bfloat16),
                grown.astype(jnp.bfloat16),
                preferred_element_type=jnp.float32,
            )

    own_ask.wait()
    widen.wait()
    for other in others:
        ask_copy(other, me).wait_recv()
        to_smem = pltpu.make_async_copy(asked.at[other], asked_smem.at[other], smem_sem.at[other])
        to_smem.start()
        to_smem.wait()

    def code_and_send(group, c, way):
        for p in range(2):
            mixed = sums[group, c, p]
            largest = jnp.max(jnp.abs(mixed), axis=0, keepdims=True)
            coded = jnp.round(mixed * (FULL / jnp.maximum(largest, 1e-30)))
            part_out[group, c, p] = coded.astype(jnp.int32).astype(jnp.int16)
            stat_out[group, c, p * 4 : p * 4 + 2, :] = sum_stat[group, c, p * 4 : p * 4 + 2, :]
            stat_out[group, c, p * 4 + 2 : p * 4 + 3, :] = largest * (1.0 / FULL)
            stat_out[group, c, p * 4 + 3 : p * 4 + 4, :] = jnp.zeros((1, 256), jnp.float32)
        stat_copy(group, c, way).start()
        part_copy(group, c, way).start()

    def add_incoming(group, c, way):
        stat_copy(group, c, way).wait_recv()
        part_copy(group, c, way).wait_recv()
        slot = group + count * way
        for p in range(2):
            at = p * 4
            there = stat_in[slot, c, at : at + 1, :]
            here = sum_stat[group, c, at : at + 1, :]
            peak = jnp.maximum(here, there)
            keep, add = jnp.exp(here - peak), jnp.exp(there - peak)
            sum_stat[group, c, at : at + 1, :] = peak
            sum_stat[group, c, at + 1 : at + 2, :] = (
                sum_stat[group, c, at + 1 : at + 2, :] * keep
                + stat_in[slot, c, at + 1 : at + 2, :] * add
            )
            part = part_in[slot, c, p].astype(jnp.int32).astype(jnp.float32)
            sums[group, c, p] = sums[group, c, p] * keep + part * (
                add * stat_in[slot, c, at + 2 : at + 3, :]
            )

    def attend(group, c):
        query_now[...] = query_slots[group, c]
        codes = [asked_smem[group, 0, j] for j in range(capacity)]
        slots = [code // 2 for code in codes]
        prompts = [code % 2 for code in codes]
        peaks = [jnp.full((1, 256), LOW, jnp.float32) for _ in range(2)]
        for j in range(capacity):
            key_scale = scale_ref[c, 0, slots[j]] * factor
            part = nt_dot(keys[slots[j], c], query_now[prompts[j]]) * key_scale
            scores[j] = part
            peak = jnp.max(part, axis=0, keepdims=True)
            for p in range(2):
                peaks[p] = jnp.maximum(peaks[p], jnp.where(prompts[j] == p, peak, LOW))
        totals = [jnp.zeros((1, 256), jnp.float32) for _ in range(2)]
        sums[group, c] = jnp.zeros((2, 128, 256), jnp.float32)
        for j in range(capacity):
            peak = jnp.where(prompts[j] == 0, peaks[0], peaks[1])
            grown = jnp.exp(scores[j] - peak)
            total = jnp.sum(grown, axis=0, keepdims=True)
            mixed = jnp.dot(
                values[slots[j], c],
                grown.astype(jnp.bfloat16),
                preferred_element_type=jnp.float32,
            )
            value_scale = scale_ref[c, 1, slots[j]]
            for p in range(2):
                totals[p] = totals[p] + jnp.where(prompts[j] == p, total, 0.0)
                sums[group, c, p] = sums[group, c, p] + mixed * jnp.where(prompts[j] == p, value_scale, 0.0)
        for p in range(2):
            sum_stat[group, c, p * 4 : p * 4 + 1, :] = peaks[p]
            sum_stat[group, c, p * 4 + 1 : p * 4 + 2, :] = totals[p]

    def serve(group, c, way):
        attend(group, c)

        @pl.when(jnp.logical_not(has_next(way)))
        def _():
            code_and_send(group, c, 1 - way)

    def serve_near(taken, index, carry):
        way = index % 2
        group = me - (1 - 2 * way) * (1 + index // 2)

        @pl.when((group >= 0) & (group < count))
        def _():
            if not taken:
                take_queries(group, 0, way)
            serve(group, 0, way)

        return carry

    def serve_far(behind, index, carry):
        way, distance = index % 2, 1 + index // 2
        group = me - (1 - 2 * way) * distance

        @pl.when(group == behind * (1 - 2 * way) + (count - 1) * way)
        def _():
            take_queries(group, 1, way)
            send_queries(1, way, distance == 1)
            serve(group, 1, way)

        return carry

    def pass_on(c, passed):
        distances = range(1, count - passed)
        for distance in distances if c == 0 else reversed(distances):
            for way in range(2):
                group = me + (1 - 2 * way) * distance
                behind = me if way == 0 else count - 1 - me

                @pl.when((group >= 0) & (group < count) & (behind == passed))
                def _(way=way, group=group):
                    add_incoming(group, c, way)
                    code_and_send(group, c, way)

    def finish(c):
        for way in range(2):

            @pl.when(has_next(1 - way))
            def _(way=way):
                add_incoming(me, c, way)

        for p in range(2):
            at = p * 4
            here = sum_stat[me, c, at : at + 1, :]
            local_peak = local_stat[c, p, 0:1, :]
            peak = jnp.maximum(here, local_peak)
            keep, add = jnp.exp(here - peak), jnp.exp(local_peak - peak)
            total = keep * sum_stat[me, c, at + 1 : at + 2, :] + add * local_stat[c, p, 1:2, :]
            mixed = sums[me, c, p] * (keep / total) + local_sum[c, p] * (add / total)
            turned[p, c] = mixed.T.reshape(2, 16, 8, 128)

    def attend_own(c, carry):
        attend(me, c)
        return carry

    lax.fori_loop(0, 2, attend_own, 0)
    taken = 2 * min(2, count - 1)
    lax.fori_loop(0, taken, functools.partial(serve_near, True), 0)
    lax.fori_loop(taken, 2 * (count - 1), functools.partial(serve_near, False), 0)
    for behind in range(count - 1):
        lax.fori_loop(0, 2 * (count - 1 - behind), functools.partial(serve_far, behind), 0)
        if behind + 1 < count - 1:
            pass_on(0, behind + 1)
    finish(0)
    for passed in range(1, count - 1):
        pass_on(1, passed)
    finish(1)
    for p in range(2):
        both = jnp.concatenate([turned[p, 0], turned[p, 1]], axis=2)
        out_ref[:, p * 16 : p * 16 + 16] = both.astype(jnp.bfloat16)

    for other in others:
        ask_copy(me, other).wait_send()
    for c in range(2):
        for way in range(2):
            for distance in range(count):
                group = me - distance if way == 0 else me + distance

                @pl.when((group >= 0) & (group < count) & has_next(way))
                def _(way=way, group=group, c=c):
                    query_copy(group, c, way).wait_send()

                target = me + distance if way == 0 else me - distance
                if distance > 0:

                    @pl.when((target >= 0) & (target < count))
                    def _(way=way, target=target, c=c):
                        stat_copy(target, c, way).wait_send()
                        part_copy(target, c, way).wait_send()


def move_queries(
    page_pool, page_scales, queries, new_entries, token_cache, cache_fill, page_counts, page_table
):
    count = lax.axis_size("pre")
    pool_rows = page_pool.shape[0]
    capacity = pool_rows // count
    width = queries.shape[-1]
    vmem = pl.BlockSpec(memory_space=pltpu.VMEM)
    hbm = pl.BlockSpec(memory_space=pltpu.HBM)
    dma = pltpu.SemaphoreType.DMA
    f32, bf16 = jnp.float32, jnp.bfloat16
    return pl.pallas_call(
        functools.partial(attend_kernel, (count, capacity, 1.0 / math.sqrt(width))),
        out_shape=jax.ShapeDtypeStruct(queries.shape, queries.dtype),
        in_specs=[hbm] * 8,
        out_specs=vmem,
        scratch_shapes=[
            pltpu.SMEM(page_counts.shape, jnp.int32),
            pltpu.SMEM(page_table.shape, jnp.int32),
            pltpu.VMEM((2, 2, pool_rows), bf16),
            pltpu.VMEM((2, 2, pool_rows), f32),
            pltpu.SMEM((2, 2, pool_rows), f32),
            pltpu.SMEM(cache_fill.shape, jnp.int32),
            pltpu.VMEM(queries.shape, bf16),
            pltpu.VMEM((512, 128), bf16),
            pltpu.VMEM((256, 128), bf16),
            pltpu.VMEM((count, 1, 128), jnp.int32),
            pltpu.VMEM((pool_rows, 512, 128), bf16),
            pltpu.VMEM((pool_rows, 2, 128, 128), bf16),
            pltpu.VMEM((pool_rows, 2, 128, 128), bf16),
            pltpu.VMEM((count, 1, 128), jnp.int32),
            pltpu.SMEM((count, 1, 128), jnp.int32),
            pltpu.VMEM((count, 2, 2, 256, 128), bf16),
            pltpu.VMEM((2, 256, 128), bf16),
            pltpu.VMEM((capacity, 128, 256), f32),
            pltpu.VMEM((count, 2, 2, 128, 256), f32),
            pltpu.VMEM((count, 2, 8, 256), f32),
            pltpu.VMEM((count, 2, 2, 128, 256), jnp.int16),
            pltpu.VMEM((2 * count, 2, 2, 128, 256), jnp.int16),
            pltpu.VMEM((count, 2, 8, 256), f32),
            pltpu.VMEM((2 * count, 2, 8, 256), f32),
            pltpu.VMEM((2, 2, 128, 256), f32),
            pltpu.VMEM((2, 2, 8, 256), f32),
            pltpu.VMEM((2, 2, 2, 16, 8, 128), f32),
            dma((8,)),
            dma((count,)),
            dma((count,)),
            dma((count,)),
            dma((count, 2, 2)),
            dma((count, 2)),
            dma((count, 2)),
            dma((2 * count, 2)),
            dma((count, 2)),
            dma((2 * count, 2)),
        ],
        compiler_params=pltpu.CompilerParams(
            collective_id=0, has_side_effects=True, vmem_limit_bytes=62 * 1024 * 1024
        ),
    )(
        page_counts,
        page_table,
        page_scales.transpose(1, 2, 0),
        cache_fill,
        queries,
        token_cache.reshape(-1, width),
        new_entries.reshape(-1, width),
        page_pool.reshape(pool_rows, -1, width),
    )


def shards(
    page_pool, page_scales, queries, new_entries, token_cache, cache_fill, page_counts, page_table
):
    args = (
        page_pool, page_scales, queries, new_entries, token_cache, cache_fill, page_counts, page_table,
    )
    count = lax.axis_size("pre")
    capacity = page_pool.shape[0] // count
    if count in (2, 4, 8) and page_pool.shape[0] % (4 * count) == 0 and capacity * page_pool[0].size > 2 * queries.size:
        return move_queries(*args)
    return move_pages(*args)


def solution(mesh):
    in_specs = (
        P(("groups", "pre"), None, "dec", None, None),
        P(("groups", "pre"), "dec", None),
        P(None, ("groups", "pre"), "dec", None),
        P(None, ("groups", "pre"), "dec", None, None),
        P(("groups", "pre"), None, "dec", None, None),
        P(("groups", "pre")),
        P(("groups", "pre"), None),
        P(("groups", "pre"), None, None),
    )
    out_specs = P(None, ("groups", "pre"), "dec", None)
    return jax.shard_map(shards, mesh=mesh, in_specs=in_specs, out_specs=out_specs, check_vma=False)
```

```python
import functools
import math

import jax
import jax.numpy as jnp
from jax import lax
from jax.experimental import pallas as pl
from jax.experimental.pallas import tpu as pltpu
from jax.sharding import PartitionSpec as P


def local_scores(grouped, cache_keys, fresh_keys, cache_fill, factor):
    cache_len = cache_keys.shape[2]
    step_count = fresh_keys.shape[1]
    cache_scores = (
        jnp.einsum("pctsgd,psicd->pctsgi", grouped, cache_keys, preferred_element_type=jnp.float32)
        * factor
    )
    present = (
        jnp.arange(cache_len, dtype=jnp.int32)[None, None, None, None, None, :]
        < cache_fill[:, None, None, :, None, None]
    )
    cache_scores = jnp.where(present, cache_scores, -jnp.inf)
    fresh_scores = (
        jnp.einsum("pctsgd,puscd->pctsgu", grouped, fresh_keys, preferred_element_type=jnp.float32)
        * factor
    )
    earlier = (
        jnp.arange(step_count, dtype=jnp.int32)[:, None]
        >= jnp.arange(step_count, dtype=jnp.int32)[None, :]
    )
    fresh_scores = jnp.where(earlier[None, None, :, None, None, :], fresh_scores, -jnp.inf)
    return (cache_scores, fresh_scores)


def local_terms(row_peak, cache_scores, fresh_scores, cache_values, fresh_values):
    cache_exp = jnp.exp(cache_scores - row_peak[..., None])
    fresh_exp = jnp.exp(fresh_scores - row_peak[..., None])
    denominator = jnp.sum(cache_exp, axis=-1) + jnp.sum(fresh_exp, axis=-1)
    mixed = jnp.einsum(
        "pctsgi,psicd->pctsgd",
        cache_exp.astype(jnp.bfloat16),
        cache_values,
        preferred_element_type=jnp.float32,
    )
    mixed = mixed + jnp.einsum(
        "pctsgu,puscd->pctsgd",
        fresh_exp.astype(jnp.bfloat16),
        fresh_values,
        preferred_element_type=jnp.float32,
    )
    return (denominator, mixed)


def request_table(group_table, lengths, pool_rows, pre_count, capacity):
    prompts, page_most = group_table.shape
    is_live = lax.broadcasted_iota(jnp.int32, (prompts, page_most), 1) < lengths[:, None]
    flat_ids = jnp.where(is_live, group_table, 0).reshape(-1)
    flat_live = is_live.reshape(-1)
    owners = jnp.where(flat_live, flat_ids // pool_rows, -1)
    pool_slots = flat_ids % pool_rows
    owner_hit = (owners[:, None] == lax.broadcasted_iota(jnp.int32, (1, pre_count), 1)).astype(
        jnp.int32
    )
    before = jnp.cumsum(owner_hit, axis=0) - owner_hit
    owner_rank = jnp.sum(before * owner_hit, axis=1)
    rank_hit = (owner_rank[:, None] == lax.broadcasted_iota(jnp.int32, (1, capacity), 1)).astype(
        jnp.int32
    )
    wanted = owner_hit[:, :, None] * rank_hit[:, None, :]
    requests = jnp.sum(wanted * (pool_slots + 1)[:, None, None], axis=0) - 1
    return (requests, owners, owner_rank, flat_live)


def pick_pages(page_pool, page_scales, wanted):
    flat_rows = jnp.maximum(wanted, 0).reshape(-1)
    page_block = jnp.take(page_pool, flat_rows, axis=0).reshape(wanted.shape + page_pool.shape[1:])
    scale_block = jnp.take(page_scales, flat_rows, axis=0).reshape(
        wanted.shape + page_scales.shape[1:]
    )
    return (page_block, scale_block)


def move_pages(
    page_pool, page_scales, queries, new_entries, token_cache, cache_fill, page_counts, page_table
):
    pre_count = lax.axis_size("pre")
    pool_rows = page_pool.shape[0]
    capacity = max(1, pool_rows // pre_count)
    kv_count = page_pool.shape[2]
    step_count, row_count, head_count, head_width = queries.shape
    prompts = page_counts.shape[1]
    page_most = page_table.shape[2]
    samples = row_count // prompts
    cache_len = token_cache.shape[1]
    head_ratio = head_count // kv_count
    factor = 1.0 / math.sqrt(head_width)
    requests, owners, owner_rank, flat_live = request_table(
        page_table[0], page_counts[0], pool_rows, pre_count, capacity
    )
    incoming = lax.all_to_all(requests, "pre", split_axis=0, concat_axis=0, tiled=True)
    page_block, scale_block = pick_pages(page_pool, page_scales, incoming)
    arrived, arrived_scales = (
        lax.all_to_all(page_block, "pre", split_axis=0, concat_axis=0, tiled=True),
        lax.all_to_all(scale_block, "pre", split_axis=0, concat_axis=0, tiled=True),
    )
    places = owners * capacity + owner_rank
    places = jnp.where(flat_live, places, 0)
    arrived = arrived.reshape((-1,) + page_pool.shape[1:])
    arrived_scales = arrived_scales.reshape((-1,) + page_scales.shape[1:])
    grouped = queries.reshape(
        step_count, prompts, samples, kv_count, head_ratio, head_width
    ).transpose(1, 3, 0, 2, 4, 5)
    cache_all = token_cache.reshape(prompts, samples, cache_len, kv_count, 2, head_width)
    fresh_all = new_entries.reshape(
        step_count, prompts, samples, kv_count, 2, head_width
    ).transpose(1, 0, 2, 3, 4, 5)
    filled = cache_fill.reshape(prompts, samples)
    cache_values = cache_all[..., 1, :]
    fresh_values = fresh_all[..., 1, :]
    cache_scores, fresh_scores = local_scores(
        grouped, cache_all[..., 0, :], fresh_all[..., 0, :], filled, factor
    )
    page_spots = places.reshape(prompts, page_most)
    live_pages = flat_live.reshape(prompts, page_most)

    def prompt_block(inputs):
        page_spot, live_row, prompt_query, cache_part, fresh_part, cache_vals, fresh_vals = inputs
        chosen = jnp.take(arrived, page_spot, axis=0)
        chosen_scales = jnp.take(arrived_scales, page_spot, axis=0).astype(jnp.float32)
        key_scale = chosen_scales[:, :, 0].T[:, None, None, None, :, None]
        prefix_scores = (
            jnp.einsum(
                "ctsgd,jicd->ctsgji",
                prompt_query,
                chosen[:, :, :, 0, :],
                preferred_element_type=jnp.float32,
            )
            * factor
            * key_scale
        )
        prefix_scores = jnp.where(live_row[:, None], prefix_scores, -jnp.inf)
        row_peak = jnp.maximum(
            jnp.max(prefix_scores, axis=(-2, -1)),
            jnp.maximum(jnp.max(cache_part, axis=-1), jnp.max(fresh_part, axis=-1)),
        )
        denominator, mixed = local_terms(
            row_peak[None], cache_part[None], fresh_part[None], cache_vals[None], fresh_vals[None]
        )
        prefix_exp = jnp.exp(prefix_scores - row_peak[..., None, None])
        denominator = denominator[0] + jnp.sum(prefix_exp, axis=(-2, -1))
        value_scale = chosen_scales[:, :, 1].T[:, None, None, None, :, None]
        per_page = jnp.einsum(
            "ctsgji,jicd->ctsgjd",
            prefix_exp.astype(jnp.bfloat16),
            chosen[:, :, :, 1, :],
            preferred_element_type=jnp.float32,
        )
        mixed = mixed[0] + jnp.sum(per_page * value_scale, axis=-2)
        return (mixed / denominator[..., None]).astype(jnp.bfloat16)

    result = lax.map(
        prompt_block,
        (page_spots, live_pages, grouped, cache_scores, fresh_scores, cache_values, fresh_values),
    )
    return result.transpose(2, 0, 3, 1, 4, 5).reshape(step_count, row_count, head_count, head_width)


MESH = pl.DeviceIdType.MESH
LOW = -1e30
FULL = 32000.0


def wanted_slots(counts, table, pool_rows):
    prompts, page_most = table.shape[1:]
    rows = lax.broadcasted_iota(jnp.int32, (8, 128), 0)
    lanes = lax.broadcasted_iota(jnp.int32, (8, 128), 1)
    carry = (jnp.zeros((8, 128), jnp.int32), jnp.zeros((8, 128), jnp.int32))
    for prompt in range(prompts):
        length = counts[0, prompt]

        def place(j, carry, prompt=prompt, length=length):
            listed, ranks = carry
            page = table[0, prompt, j]
            owner = jnp.where(j < length, page // pool_rows, -1)
            hit = rows == owner
            code = (page - owner * pool_rows) * 2 + prompt
            listed = jnp.where(hit & (ranks == lanes), code, listed)
            return listed, jnp.where(hit, ranks + 1, ranks)

        carry = lax.fori_loop(0, page_most, place, carry)
    return carry[0]


def nt_dot(a, b):
    return lax.dot_general(a, b, (((1,), (1,)), ((), ())), preferred_element_type=jnp.float32)


def attend_kernel(
    dims,
    counts_hbm,
    table_hbm,
    scale_hbm,
    fill_hbm,
    queries_hbm,
    cache_hbm,
    fresh_hbm,
    pool_hbm,
    out_ref,
    counts_ref,
    table_ref,
    scale_raw,
    scale_wide,
    scale_ref,
    fill_ref,
    queries_ref,
    cache_ref,
    fresh_ref,
    request_ref,
    raw,
    keys,
    values,
    asked,
    asked_smem,
    query_slots,
    query_now,
    scores,
    sums,
    sum_stat,
    part_out,
    part_in,
    stat_out,
    stat_in,
    local_sum,
    local_stat,
    turned,
    load_sem,
    smem_sem,
    ask_send,
    ask_recv,
    query_send,
    query_recv,
    part_send,
    part_recv,
    stat_send,
    stat_recv,
):
    count, capacity, factor = dims
    pages = raw.shape[0]
    me = lax.axis_index("pre")
    others = [lax.rem(me + k, count) for k in range(1, count)]

    barrier = pltpu.get_barrier_semaphore()
    for other in others:
        pl.semaphore_signal(barrier, inc=1, device_id={"pre": other}, device_id_type=MESH)
    pairs = (
        (queries_hbm, queries_ref),
        (table_hbm, table_ref),
        (counts_hbm, counts_ref),
        (fresh_hbm, fresh_ref),
        (cache_hbm, cache_ref),
        (fill_hbm, fill_ref),
        (scale_hbm, scale_raw),
        (pool_hbm, raw),
    )
    loads = [pltpu.make_async_copy(a, b, load_sem.at[i]) for i, (a, b) in enumerate(pairs)]
    for load in loads:
        load.start()
    load_queries, load_table, load_counts, load_fresh, load_cache, load_fill, load_scale, load_pool = loads
    load_queries.wait()
    for prompt in range(2):
        for step in range(2):
            block = queries_ref[step, prompt * 16 : prompt * 16 + 16].astype(jnp.float32)
            for c in range(2):
                rows = block[:, c * 8 : c * 8 + 8, :].reshape(128, 128)
                query_slots[me, c, prompt, step * 128 : step * 128 + 128, :] = rows.astype(
                    jnp.bfloat16
                )
    pl.semaphore_wait(barrier, count - 1)

    def ask_copy(source, target):
        return pltpu.make_async_remote_copy(
            src_ref=request_ref.at[target],
            dst_ref=asked.at[source],
            send_sem=ask_send.at[target],
            recv_sem=ask_recv.at[source],
            device_id={"pre": target},
            device_id_type=MESH,
        )

    def query_copy(group, c, way):
        return pltpu.make_async_remote_copy(
            src_ref=query_slots.at[group, c],
            dst_ref=query_slots.at[group, c],
            send_sem=query_send.at[group, c, way],
            recv_sem=query_recv.at[group, c],
            device_id={"pre": me + 1 - 2 * way},
            device_id_type=MESH,
        )

    def part_copy(group, c, way):
        return pltpu.make_async_remote_copy(
            src_ref=part_out.at[group, c],
            dst_ref=part_in.at[group + count * way, c],
            send_sem=part_send.at[group, c],
            recv_sem=part_recv.at[group + count * way, c],
            device_id={"pre": me + 1 - 2 * way},
            device_id_type=MESH,
        )

    def stat_copy(group, c, way):
        return pltpu.make_async_remote_copy(
            src_ref=stat_out.at[group, c],
            dst_ref=stat_in.at[group + count * way, c],
            send_sem=stat_send.at[group, c],
            recv_sem=stat_recv.at[group + count * way, c],
            device_id={"pre": me + 1 - 2 * way},
            device_id_type=MESH,
        )

    def has_next(way):
        ahead = me + 1 - 2 * way
        return (ahead >= 0) & (ahead < count)

    def send_queries(c, way):
        @pl.when(has_next(way))
        def _():
            query_copy(me, c, way).start()

    def take_queries(group, c, way):
        query_copy(group, c, way).wait_recv()

        @pl.when(has_next(way))
        def _():
            query_copy(group, c, way).start()

    for c in range(2):
        for way in range(2):
            send_queries(c, way)
    load_table.wait()
    load_counts.wait()
    listed = wanted_slots(counts_ref, table_ref, pages)
    for owner in range(count):
        request_ref[owner] = listed[owner : owner + 1]
    for other in others:
        ask_copy(me, other).start()
    own_ask = pltpu.make_async_copy(request_ref.at[me], asked_smem.at[me], smem_sem.at[me])
    own_ask.start()
    load_scale.wait()
    scale_wide[...] = scale_raw[...].astype(jnp.float32)
    widen = pltpu.make_async_copy(scale_wide, scale_ref, load_sem.at[6])
    widen.start()
    load_fresh.wait()
    load_cache.wait()
    load_fill.wait()

    to_row = lax.broadcasted_iota(jnp.int32, (256, 256), 0)
    from_row = lax.broadcasted_iota(jnp.int32, (256, 256), 1)
    order = jnp.where(from_row == (to_row % 64) * 4 + to_row // 64, 1.0, 0.0).astype(jnp.bfloat16)

    def sort_rows(block):
        return jnp.dot(order, block, preferred_element_type=jnp.float32)

    load_pool.wait()

    def sort_pages(block, carry):
        for i in range(4):
            page = block * 4 + i
            sides = jnp.concatenate([raw[page, :256, :], raw[page, 256:, :]], axis=1)
            rows = sort_rows(sides)
            for c in range(2):
                at = c * 128
                keys[page, c, :64] = rows[at : at + 64, :128].astype(jnp.bfloat16)
                keys[page, c, 64:] = rows[at : at + 64, 128:].astype(jnp.bfloat16)
                held = rows[at + 64 : at + 128]
                values[page, c] = jnp.concatenate(
                    [held[:, :128], held[:, 128:]], axis=0
                ).T.astype(jnp.bfloat16)
        return carry

    blocks = pages // 4
    def take_all(distance, c):
        for way in range(2):
            group = me - (1 - 2 * way) * distance

            @pl.when((group >= 0) & (group < count))
            def _(way=way, group=group):
                take_queries(group, c, way)

    lax.fori_loop(0, blocks // 2, sort_pages, 0)
    take_all(1, 0)
    lax.fori_loop(blocks // 2, blocks, sort_pages, 0)
    take_all(1, 1)
    if count > 2:
        take_all(2, 0)

    fresh_block = jnp.concatenate(
        [
            fresh_ref[step * 128 + prompt * 64 : step * 128 + prompt * 64 + 64, :]
            for prompt in range(2)
            for step in range(2)
        ],
        axis=0,
    )
    fresh_rows = sort_rows(fresh_block)
    key_at = lax.broadcasted_iota(jnp.int32, (128, 256), 0)
    query_at = lax.broadcasted_iota(jnp.int32, (128, 256), 1)
    query_sample = (query_at // 8) % 16
    is_cache = key_at < 64
    is_fresh = (key_at >= 64) & (key_at < 96)
    fresh_ok = is_fresh & (key_at % 16 == query_sample) & ((key_at - 64) // 16 <= query_at // 128)
    cache_same = is_cache & (key_at // 4 == query_sample)
    for prompt in range(2):
        cache_rows = sort_rows(cache_ref[prompt * 256 : prompt * 256 + 256, :])
        filled = jnp.zeros((128, 256), jnp.int32)
        for sample in range(16):
            filled = jnp.where(query_sample == sample, fill_ref[prompt * 16 + sample], filled)
        present = (cache_same & (key_at % 4 < filled)) | fresh_ok
        for c in range(2):

            def pick(kind):
                at = (c * 2 + kind) * 64
                return jnp.concatenate(
                    [
                        cache_rows[at : at + 64],
                        fresh_rows[at + prompt * 32 : at + prompt * 32 + 32],
                        jnp.zeros((32, 128), jnp.float32),
                    ],
                    axis=0,
                )

            part = nt_dot(pick(0).astype(jnp.bfloat16), query_slots[me, c, prompt]) * factor
            part = jnp.where(present, part, LOW)
            peak = jnp.max(part, axis=0, keepdims=True)
            grown = jnp.exp(part - peak)
            local_stat[c, prompt, 0:1, :] = peak
            local_stat[c, prompt, 1:2, :] = jnp.sum(grown, axis=0, keepdims=True)
            local_sum[c, prompt] = jnp.dot(
                pick(1).T.astype(jnp.bfloat16),
                grown.astype(jnp.bfloat16),
                preferred_element_type=jnp.float32,
            )

    own_ask.wait()
    widen.wait()
    for other in others:
        ask_copy(other, me).wait_recv()
        to_smem = pltpu.make_async_copy(asked.at[other], asked_smem.at[other], smem_sem.at[other])
        to_smem.start()
        to_smem.wait()

    def code_and_send(group, c, way):
        for p in range(2):
            mixed = sums[group, c, p]
            largest = jnp.max(jnp.abs(mixed), axis=0, keepdims=True)
            coded = jnp.round(mixed * (FULL / jnp.maximum(largest, 1e-30)))
            part_out[group, c, p] = coded.astype(jnp.int32).astype(jnp.int16)
            stat_out[group, c, p * 4 : p * 4 + 2, :] = sum_stat[group, c, p * 4 : p * 4 + 2, :]
            stat_out[group, c, p * 4 + 2 : p * 4 + 3, :] = largest * (1.0 / FULL)
            stat_out[group, c, p * 4 + 3 : p * 4 + 4, :] = jnp.zeros((1, 256), jnp.float32)
        stat_copy(group, c, way).start()
        part_copy(group, c, way).start()

    def add_incoming(group, c, way):
        stat_copy(group, c, way).wait_recv()
        part_copy(group, c, way).wait_recv()
        slot = group + count * way
        for p in range(2):
            at = p * 4
            there = stat_in[slot, c, at : at + 1, :]
            here = sum_stat[group, c, at : at + 1, :]
            peak = jnp.maximum(here, there)
            keep, add = jnp.exp(here - peak), jnp.exp(there - peak)
            sum_stat[group, c, at : at + 1, :] = peak
            sum_stat[group, c, at + 1 : at + 2, :] = (
                sum_stat[group, c, at + 1 : at + 2, :] * keep
                + stat_in[slot, c, at + 1 : at + 2, :] * add
            )
            part = part_in[slot, c, p].astype(jnp.int32).astype(jnp.float32)
            sums[group, c, p] = sums[group, c, p] * keep + part * (
                add * stat_in[slot, c, at + 2 : at + 3, :]
            )

    def attend(group, c):
        query_now[...] = query_slots[group, c]
        codes = [asked_smem[group, 0, j] for j in range(capacity)]
        slots = [code // 2 for code in codes]
        prompts = [code % 2 for code in codes]
        peaks = [jnp.full((1, 256), LOW, jnp.float32) for _ in range(2)]
        for j in range(capacity):
            key_scale = scale_ref[c, 0, slots[j]] * factor
            part = nt_dot(keys[slots[j], c], query_now[prompts[j]]) * key_scale
            scores[j] = part
            peak = jnp.max(part, axis=0, keepdims=True)
            for p in range(2):
                peaks[p] = jnp.maximum(peaks[p], jnp.where(prompts[j] == p, peak, LOW))
        totals = [jnp.zeros((1, 256), jnp.float32) for _ in range(2)]
        sums[group, c] = jnp.zeros((2, 128, 256), jnp.float32)
        for j in range(capacity):
            peak = jnp.where(prompts[j] == 0, peaks[0], peaks[1])
            grown = jnp.exp(scores[j] - peak)
            total = jnp.sum(grown, axis=0, keepdims=True)
            mixed = jnp.dot(
                values[slots[j], c],
                grown.astype(jnp.bfloat16),
                preferred_element_type=jnp.float32,
            )
            value_scale = scale_ref[c, 1, slots[j]]
            for p in range(2):
                totals[p] = totals[p] + jnp.where(prompts[j] == p, total, 0.0)
                sums[group, c, p] = sums[group, c, p] + mixed * jnp.where(prompts[j] == p, value_scale, 0.0)
        for p in range(2):
            sum_stat[group, c, p * 4 : p * 4 + 1, :] = peaks[p]
            sum_stat[group, c, p * 4 + 1 : p * 4 + 2, :] = totals[p]

    def serve(group, c, way):
        attend(group, c)

        @pl.when(jnp.logical_not(has_next(way)))
        def _():
            code_and_send(group, c, 1 - way)

    def serve_next(index, carry):
        distance, c, way = 1 + index // 4, index // 2 % 2, index % 2
        group = me - (1 - 2 * way) * distance

        @pl.when((group >= 0) & (group < count))
        def _():
            @pl.when(distance * 2 + c > 4)
            def _():
                take_queries(group, c, way)

            serve(group, c, way)

        return carry

    def pass_on(c, passed, distance):
        for way in range(2):
            group = me + (1 - 2 * way) * distance
            behind = me if way == 0 else count - 1 - me

            @pl.when((group >= 0) & (group < count) & (behind == passed))
            def _(way=way, group=group):
                add_incoming(group, c, way)
                code_and_send(group, c, way)

    def finish(c):
        for way in range(2):

            @pl.when(has_next(1 - way))
            def _(way=way):
                add_incoming(me, c, way)

        for p in range(2):
            at = p * 4
            here = sum_stat[me, c, at : at + 1, :]
            local_peak = local_stat[c, p, 0:1, :]
            peak = jnp.maximum(here, local_peak)
            keep, add = jnp.exp(here - peak), jnp.exp(local_peak - peak)
            total = keep * sum_stat[me, c, at + 1 : at + 2, :] + add * local_stat[c, p, 1:2, :]
            mixed = sums[me, c, p] * (keep / total) + local_sum[c, p] * (add / total)
            turned[p, c] = mixed.T.reshape(2, 16, 8, 128)

    def attend_own(c, carry):
        attend(me, c)
        return carry

    lax.fori_loop(0, 2, attend_own, 0)
    lax.fori_loop(0, 4 * (count - 1), serve_next, 0)
    for passed in range(1, count - 1):
        for distance in range(1, count - passed):
            for c in range(2):
                pass_on(c, passed, distance)
    finish(0)
    finish(1)
    for p in range(2):
        both = jnp.concatenate([turned[p, 0], turned[p, 1]], axis=2)
        out_ref[:, p * 16 : p * 16 + 16] = both.astype(jnp.bfloat16)

    for other in others:
        ask_copy(me, other).wait_send()
    for c in range(2):
        for way in range(2):
            for distance in range(count):
                group = me - distance if way == 0 else me + distance

                @pl.when((group >= 0) & (group < count) & has_next(way))
                def _(way=way, group=group, c=c):
                    query_copy(group, c, way).wait_send()

                target = me + distance if way == 0 else me - distance
                if distance > 0:

                    @pl.when((target >= 0) & (target < count))
                    def _(way=way, target=target, c=c):
                        stat_copy(target, c, way).wait_send()
                        part_copy(target, c, way).wait_send()


def move_queries(
    page_pool, page_scales, queries, new_entries, token_cache, cache_fill, page_counts, page_table
):
    count = lax.axis_size("pre")
    pool_rows = page_pool.shape[0]
    capacity = pool_rows // count
    width = queries.shape[-1]
    vmem = pl.BlockSpec(memory_space=pltpu.VMEM)
    hbm = pl.BlockSpec(memory_space=pltpu.HBM)
    dma = pltpu.SemaphoreType.DMA
    f32, bf16 = jnp.float32, jnp.bfloat16
    return pl.pallas_call(
        functools.partial(attend_kernel, (count, capacity, 1.0 / math.sqrt(width))),
        out_shape=jax.ShapeDtypeStruct(queries.shape, queries.dtype),
        in_specs=[hbm] * 8,
        out_specs=vmem,
        scratch_shapes=[
            pltpu.SMEM(page_counts.shape, jnp.int32),
            pltpu.SMEM(page_table.shape, jnp.int32),
            pltpu.VMEM((2, 2, pool_rows), bf16),
            pltpu.VMEM((2, 2, pool_rows), f32),
            pltpu.SMEM((2, 2, pool_rows), f32),
            pltpu.SMEM(cache_fill.shape, jnp.int32),
            pltpu.VMEM(queries.shape, bf16),
            pltpu.VMEM((512, 128), bf16),
            pltpu.VMEM((256, 128), bf16),
            pltpu.VMEM((count, 1, 128), jnp.int32),
            pltpu.VMEM((pool_rows, 512, 128), bf16),
            pltpu.VMEM((pool_rows, 2, 128, 128), bf16),
            pltpu.VMEM((pool_rows, 2, 128, 128), bf16),
            pltpu.VMEM((count, 1, 128), jnp.int32),
            pltpu.SMEM((count, 1, 128), jnp.int32),
            pltpu.VMEM((count, 2, 2, 256, 128), bf16),
            pltpu.VMEM((2, 256, 128), bf16),
            pltpu.VMEM((capacity, 128, 256), f32),
            pltpu.VMEM((count, 2, 2, 128, 256), f32),
            pltpu.VMEM((count, 2, 8, 256), f32),
            pltpu.VMEM((count, 2, 2, 128, 256), jnp.int16),
            pltpu.VMEM((2 * count, 2, 2, 128, 256), jnp.int16),
            pltpu.VMEM((count, 2, 8, 256), f32),
            pltpu.VMEM((2 * count, 2, 8, 256), f32),
            pltpu.VMEM((2, 2, 128, 256), f32),
            pltpu.VMEM((2, 2, 8, 256), f32),
            pltpu.VMEM((2, 2, 2, 16, 8, 128), f32),
            dma((8,)),
            dma((count,)),
            dma((count,)),
            dma((count,)),
            dma((count, 2, 2)),
            dma((count, 2)),
            dma((count, 2)),
            dma((2 * count, 2)),
            dma((count, 2)),
            dma((2 * count, 2)),
        ],
        compiler_params=pltpu.CompilerParams(
            collective_id=0, has_side_effects=True, vmem_limit_bytes=62 * 1024 * 1024
        ),
    )(
        page_counts,
        page_table,
        page_scales.transpose(1, 2, 0),
        cache_fill,
        queries,
        token_cache.reshape(-1, width),
        new_entries.reshape(-1, width),
        page_pool.reshape(pool_rows, -1, width),
    )


def shards(
    page_pool, page_scales, queries, new_entries, token_cache, cache_fill, page_counts, page_table
):
    args = (
        page_pool, page_scales, queries, new_entries, token_cache, cache_fill, page_counts, page_table,
    )
    count = lax.axis_size("pre")
    capacity = page_pool.shape[0] // count
    if count in (2, 4, 8) and page_pool.shape[0] % (4 * count) == 0 and capacity * page_pool[0].size > 2 * queries.size:
        return move_queries(*args)
    return move_pages(*args)


def solution(mesh):
    in_specs = (
        P(("groups", "pre"), None, "dec", None, None),
        P(("groups", "pre"), "dec", None),
        P(None, ("groups", "pre"), "dec", None),
        P(None, ("groups", "pre"), "dec", None, None),
        P(("groups", "pre"), None, "dec", None, None),
        P(("groups", "pre")),
        P(("groups", "pre"), None),
        P(("groups", "pre"), None, None),
    )
    out_specs = P(None, ("groups", "pre"), "dec", None)
    return jax.shard_map(shards, mesh=mesh, in_specs=in_specs, out_specs=out_specs, check_vma=False)
```

```python
import functools
import math

import jax
import jax.numpy as jnp
from jax import lax
from jax.experimental import pallas as pl
from jax.experimental.pallas import tpu as pltpu
from jax.sharding import PartitionSpec as P


def local_scores(grouped, cache_keys, fresh_keys, cache_fill, factor):
    cache_len = cache_keys.shape[2]
    step_count = fresh_keys.shape[1]
    cache_scores = (
        jnp.einsum("pctsgd,psicd->pctsgi", grouped, cache_keys, preferred_element_type=jnp.float32)
        * factor
    )
    present = (
        jnp.arange(cache_len, dtype=jnp.int32)[None, None, None, None, None, :]
        < cache_fill[:, None, None, :, None, None]
    )
    cache_scores = jnp.where(present, cache_scores, -jnp.inf)
    fresh_scores = (
        jnp.einsum("pctsgd,puscd->pctsgu", grouped, fresh_keys, preferred_element_type=jnp.float32)
        * factor
    )
    earlier = (
        jnp.arange(step_count, dtype=jnp.int32)[:, None]
        >= jnp.arange(step_count, dtype=jnp.int32)[None, :]
    )
    fresh_scores = jnp.where(earlier[None, None, :, None, None, :], fresh_scores, -jnp.inf)
    return (cache_scores, fresh_scores)


def local_terms(row_peak, cache_scores, fresh_scores, cache_values, fresh_values):
    cache_exp = jnp.exp(cache_scores - row_peak[..., None])
    fresh_exp = jnp.exp(fresh_scores - row_peak[..., None])
    denominator = jnp.sum(cache_exp, axis=-1) + jnp.sum(fresh_exp, axis=-1)
    mixed = jnp.einsum(
        "pctsgi,psicd->pctsgd",
        cache_exp.astype(jnp.bfloat16),
        cache_values,
        preferred_element_type=jnp.float32,
    )
    mixed = mixed + jnp.einsum(
        "pctsgu,puscd->pctsgd",
        fresh_exp.astype(jnp.bfloat16),
        fresh_values,
        preferred_element_type=jnp.float32,
    )
    return (denominator, mixed)


def request_table(group_table, lengths, pool_rows, pre_count, capacity):
    prompts, page_most = group_table.shape
    is_live = lax.broadcasted_iota(jnp.int32, (prompts, page_most), 1) < lengths[:, None]
    flat_ids = jnp.where(is_live, group_table, 0).reshape(-1)
    flat_live = is_live.reshape(-1)
    owners = jnp.where(flat_live, flat_ids // pool_rows, -1)
    pool_slots = flat_ids % pool_rows
    owner_hit = (owners[:, None] == lax.broadcasted_iota(jnp.int32, (1, pre_count), 1)).astype(
        jnp.int32
    )
    before = jnp.cumsum(owner_hit, axis=0) - owner_hit
    owner_rank = jnp.sum(before * owner_hit, axis=1)
    rank_hit = (owner_rank[:, None] == lax.broadcasted_iota(jnp.int32, (1, capacity), 1)).astype(
        jnp.int32
    )
    wanted = owner_hit[:, :, None] * rank_hit[:, None, :]
    requests = jnp.sum(wanted * (pool_slots + 1)[:, None, None], axis=0) - 1
    return (requests, owners, owner_rank, flat_live)


def pick_pages(page_pool, page_scales, wanted):
    flat_rows = jnp.maximum(wanted, 0).reshape(-1)
    page_block = jnp.take(page_pool, flat_rows, axis=0).reshape(wanted.shape + page_pool.shape[1:])
    scale_block = jnp.take(page_scales, flat_rows, axis=0).reshape(
        wanted.shape + page_scales.shape[1:]
    )
    return (page_block, scale_block)


def move_pages(
    page_pool, page_scales, queries, new_entries, token_cache, cache_fill, page_counts, page_table
):
    pre_count = lax.axis_size("pre")
    pool_rows = page_pool.shape[0]
    capacity = max(1, pool_rows // pre_count)
    kv_count = page_pool.shape[2]
    step_count, row_count, head_count, head_width = queries.shape
    prompts = page_counts.shape[1]
    page_most = page_table.shape[2]
    samples = row_count // prompts
    cache_len = token_cache.shape[1]
    head_ratio = head_count // kv_count
    factor = 1.0 / math.sqrt(head_width)
    requests, owners, owner_rank, flat_live = request_table(
        page_table[0], page_counts[0], pool_rows, pre_count, capacity
    )
    incoming = lax.all_to_all(requests, "pre", split_axis=0, concat_axis=0, tiled=True)
    page_block, scale_block = pick_pages(page_pool, page_scales, incoming)
    arrived, arrived_scales = (
        lax.all_to_all(page_block, "pre", split_axis=0, concat_axis=0, tiled=True),
        lax.all_to_all(scale_block, "pre", split_axis=0, concat_axis=0, tiled=True),
    )
    places = owners * capacity + owner_rank
    places = jnp.where(flat_live, places, 0)
    arrived = arrived.reshape((-1,) + page_pool.shape[1:])
    arrived_scales = arrived_scales.reshape((-1,) + page_scales.shape[1:])
    grouped = queries.reshape(
        step_count, prompts, samples, kv_count, head_ratio, head_width
    ).transpose(1, 3, 0, 2, 4, 5)
    cache_all = token_cache.reshape(prompts, samples, cache_len, kv_count, 2, head_width)
    fresh_all = new_entries.reshape(
        step_count, prompts, samples, kv_count, 2, head_width
    ).transpose(1, 0, 2, 3, 4, 5)
    filled = cache_fill.reshape(prompts, samples)
    cache_values = cache_all[..., 1, :]
    fresh_values = fresh_all[..., 1, :]
    cache_scores, fresh_scores = local_scores(
        grouped, cache_all[..., 0, :], fresh_all[..., 0, :], filled, factor
    )
    page_spots = places.reshape(prompts, page_most)
    live_pages = flat_live.reshape(prompts, page_most)

    def prompt_block(inputs):
        page_spot, live_row, prompt_query, cache_part, fresh_part, cache_vals, fresh_vals = inputs
        chosen = jnp.take(arrived, page_spot, axis=0)
        chosen_scales = jnp.take(arrived_scales, page_spot, axis=0).astype(jnp.float32)
        key_scale = chosen_scales[:, :, 0].T[:, None, None, None, :, None]
        prefix_scores = (
            jnp.einsum(
                "ctsgd,jicd->ctsgji",
                prompt_query,
                chosen[:, :, :, 0, :],
                preferred_element_type=jnp.float32,
            )
            * factor
            * key_scale
        )
        prefix_scores = jnp.where(live_row[:, None], prefix_scores, -jnp.inf)
        row_peak = jnp.maximum(
            jnp.max(prefix_scores, axis=(-2, -1)),
            jnp.maximum(jnp.max(cache_part, axis=-1), jnp.max(fresh_part, axis=-1)),
        )
        denominator, mixed = local_terms(
            row_peak[None], cache_part[None], fresh_part[None], cache_vals[None], fresh_vals[None]
        )
        prefix_exp = jnp.exp(prefix_scores - row_peak[..., None, None])
        denominator = denominator[0] + jnp.sum(prefix_exp, axis=(-2, -1))
        value_scale = chosen_scales[:, :, 1].T[:, None, None, None, :, None]
        per_page = jnp.einsum(
            "ctsgji,jicd->ctsgjd",
            prefix_exp.astype(jnp.bfloat16),
            chosen[:, :, :, 1, :],
            preferred_element_type=jnp.float32,
        )
        mixed = mixed[0] + jnp.sum(per_page * value_scale, axis=-2)
        return (mixed / denominator[..., None]).astype(jnp.bfloat16)

    result = lax.map(
        prompt_block,
        (page_spots, live_pages, grouped, cache_scores, fresh_scores, cache_values, fresh_values),
    )
    return result.transpose(2, 0, 3, 1, 4, 5).reshape(step_count, row_count, head_count, head_width)


MESH = pl.DeviceIdType.MESH
LOW = -1e30
FULL = 32000.0


def wanted_slots(counts, table, pool_rows):
    prompts, page_most = table.shape[1:]
    rows = lax.broadcasted_iota(jnp.int32, (8, 128), 0)
    lanes = lax.broadcasted_iota(jnp.int32, (8, 128), 1)
    carry = (jnp.zeros((8, 128), jnp.int32), jnp.zeros((8, 128), jnp.int32))
    for prompt in range(prompts):
        length = counts[0, prompt]

        def place(j, carry, prompt=prompt, length=length):
            listed, ranks = carry
            page = table[0, prompt, j]
            owner = jnp.where(j < length, page // pool_rows, -1)
            hit = rows == owner
            code = (page - owner * pool_rows) * 2 + prompt
            listed = jnp.where(hit & (ranks == lanes), code, listed)
            return listed, jnp.where(hit, ranks + 1, ranks)

        carry = lax.fori_loop(0, page_most, place, carry)
    return carry[0]


def nt_dot(a, b):
    return lax.dot_general(a, b, (((1,), (1,)), ((), ())), preferred_element_type=jnp.float32)


def attend_kernel(
    dims,
    counts_hbm,
    table_hbm,
    scale_hbm,
    fill_hbm,
    queries_hbm,
    cache_hbm,
    fresh_hbm,
    pool_hbm,
    out_ref,
    counts_ref,
    table_ref,
    scale_raw,
    scale_wide,
    scale_ref,
    fill_ref,
    queries_ref,
    cache_ref,
    fresh_ref,
    request_ref,
    raw,
    keys,
    values,
    asked,
    asked_smem,
    query_slots,
    query_now,
    scores,
    sums,
    sum_stat,
    part_out,
    part_in,
    stat_out,
    stat_in,
    local_sum,
    local_stat,
    turned,
    load_sem,
    smem_sem,
    ask_send,
    ask_recv,
    query_send,
    query_recv,
    part_send,
    part_recv,
    stat_send,
    stat_recv,
):
    count, capacity, factor = dims
    pages = raw.shape[0]
    me = lax.axis_index("pre")
    others = [lax.rem(me + k, count) for k in range(1, count)]

    barrier = pltpu.get_barrier_semaphore()
    for other in others:
        pl.semaphore_signal(barrier, inc=1, device_id={"pre": other}, device_id_type=MESH)
    pairs = (
        (queries_hbm, queries_ref),
        (table_hbm, table_ref),
        (counts_hbm, counts_ref),
        (fresh_hbm, fresh_ref),
        (cache_hbm, cache_ref),
        (fill_hbm, fill_ref),
        (scale_hbm, scale_raw),
        (pool_hbm, raw),
    )
    loads = [pltpu.make_async_copy(a, b, load_sem.at[i]) for i, (a, b) in enumerate(pairs)]
    for load in loads:
        load.start()
    load_queries, load_table, load_counts, load_fresh, load_cache, load_fill, load_scale, load_pool = loads
    load_queries.wait()
    for prompt in range(2):
        for step in range(2):
            block = queries_ref[step, prompt * 16 : prompt * 16 + 16].astype(jnp.float32)
            for c in range(2):
                rows = block[:, c * 8 : c * 8 + 8, :].reshape(128, 128)
                query_slots[me, c, prompt, step * 128 : step * 128 + 128, :] = rows.astype(
                    jnp.bfloat16
                )
    pl.semaphore_wait(barrier, count - 1)

    def ask_copy(source, target):
        return pltpu.make_async_remote_copy(
            src_ref=request_ref.at[target],
            dst_ref=asked.at[source],
            send_sem=ask_send.at[target],
            recv_sem=ask_recv.at[source],
            device_id={"pre": target},
            device_id_type=MESH,
        )

    def query_copy(group, c, target):
        return pltpu.make_async_remote_copy(
            src_ref=query_slots.at[group, c],
            dst_ref=query_slots.at[group, c],
            send_sem=query_send.at[target, c],
            recv_sem=query_recv.at[group, c],
            device_id={"pre": target},
            device_id_type=MESH,
        )

    def part_copy(group, c, way):
        return pltpu.make_async_remote_copy(
            src_ref=part_out.at[group, c],
            dst_ref=part_in.at[group + count * way, c],
            send_sem=part_send.at[group, c],
            recv_sem=part_recv.at[group + count * way, c],
            device_id={"pre": me + 1 - 2 * way},
            device_id_type=MESH,
        )

    def stat_copy(group, c, way):
        return pltpu.make_async_remote_copy(
            src_ref=stat_out.at[group, c],
            dst_ref=stat_in.at[group + count * way, c],
            send_sem=stat_send.at[group, c],
            recv_sem=stat_recv.at[group + count * way, c],
            device_id={"pre": me + 1 - 2 * way},
            device_id_type=MESH,
        )

    def has_next(way):
        ahead = me + 1 - 2 * way
        return (ahead >= 0) & (ahead < count)

    for c in range(2):
        for other in others:
            query_copy(me, c, other).start()
    load_table.wait()
    load_counts.wait()
    listed = wanted_slots(counts_ref, table_ref, pages)
    for owner in range(count):
        request_ref[owner] = listed[owner : owner + 1]
    for other in others:
        ask_copy(me, other).start()
    own_ask = pltpu.make_async_copy(request_ref.at[me], asked_smem.at[me], smem_sem.at[me])
    own_ask.start()
    load_scale.wait()
    scale_wide[...] = scale_raw[...].astype(jnp.float32)
    widen = pltpu.make_async_copy(scale_wide, scale_ref, load_sem.at[6])
    widen.start()
    load_fresh.wait()
    load_cache.wait()
    load_fill.wait()

    to_row = lax.broadcasted_iota(jnp.int32, (256, 256), 0)
    from_row = lax.broadcasted_iota(jnp.int32, (256, 256), 1)
    order = jnp.where(from_row == (to_row % 64) * 4 + to_row // 64, 1.0, 0.0).astype(jnp.bfloat16)

    def sort_rows(block):
        return jnp.dot(order, block, preferred_element_type=jnp.float32)

    load_pool.wait()

    def sort_pages(block, carry):
        for i in range(4):
            page = block * 4 + i
            sides = jnp.concatenate([raw[page, :256, :], raw[page, 256:, :]], axis=1)
            rows = sort_rows(sides)
            for c in range(2):
                at = c * 128
                keys[page, c, :64] = rows[at : at + 64, :128].astype(jnp.bfloat16)
                keys[page, c, 64:] = rows[at : at + 64, 128:].astype(jnp.bfloat16)
                held = rows[at + 64 : at + 128]
                values[page, c] = jnp.concatenate(
                    [held[:, :128], held[:, 128:]], axis=0
                ).T.astype(jnp.bfloat16)
        return carry

    blocks = pages // 4
    lax.fori_loop(0, blocks, sort_pages, 0)

    fresh_block = jnp.concatenate(
        [
            fresh_ref[step * 128 + prompt * 64 : step * 128 + prompt * 64 + 64, :]
            for prompt in range(2)
            for step in range(2)
        ],
        axis=0,
    )
    fresh_rows = sort_rows(fresh_block)
    key_at = lax.broadcasted_iota(jnp.int32, (128, 256), 0)
    query_at = lax.broadcasted_iota(jnp.int32, (128, 256), 1)
    query_sample = (query_at // 8) % 16
    is_cache = key_at < 64
    is_fresh = (key_at >= 64) & (key_at < 96)
    fresh_ok = is_fresh & (key_at % 16 == query_sample) & ((key_at - 64) // 16 <= query_at // 128)
    cache_same = is_cache & (key_at // 4 == query_sample)
    for prompt in range(2):
        cache_rows = sort_rows(cache_ref[prompt * 256 : prompt * 256 + 256, :])
        filled = jnp.zeros((128, 256), jnp.int32)
        for sample in range(16):
            filled = jnp.where(query_sample == sample, fill_ref[prompt * 16 + sample], filled)
        present = (cache_same & (key_at % 4 < filled)) | fresh_ok
        for c in range(2):

            def pick(kind):
                at = (c * 2 + kind) * 64
                return jnp.concatenate(
                    [
                        cache_rows[at : at + 64],
                        fresh_rows[at + prompt * 32 : at + prompt * 32 + 32],
                        jnp.zeros((32, 128), jnp.float32),
                    ],
                    axis=0,
                )

            part = nt_dot(pick(0).astype(jnp.bfloat16), query_slots[me, c, prompt]) * factor
            part = jnp.where(present, part, LOW)
            peak = jnp.max(part, axis=0, keepdims=True)
            grown = jnp.exp(part - peak)
            local_stat[c, prompt, 0:1, :] = peak
            local_stat[c, prompt, 1:2, :] = jnp.sum(grown, axis=0, keepdims=True)
            local_sum[c, prompt] = jnp.dot(
                pick(1).T.astype(jnp.bfloat16),
                grown.astype(jnp.bfloat16),
                preferred_element_type=jnp.float32,
            )

    own_ask.wait()
    widen.wait()
    for other in others:
        ask_copy(other, me).wait_recv()
        to_smem = pltpu.make_async_copy(asked.at[other], asked_smem.at[other], smem_sem.at[other])
        to_smem.start()
        to_smem.wait()

    def code_and_send(group, c, way):
        for p in range(2):
            mixed = sums[group, c, p]
            largest = jnp.max(jnp.abs(mixed), axis=0, keepdims=True)
            coded = jnp.round(mixed * (FULL / jnp.maximum(largest, 1e-30)))
            part_out[group, c, p] = coded.astype(jnp.int32).astype(jnp.int16)
            stat_out[group, c, p * 4 : p * 4 + 2, :] = sum_stat[group, c, p * 4 : p * 4 + 2, :]
            stat_out[group, c, p * 4 + 2 : p * 4 + 3, :] = largest * (1.0 / FULL)
            stat_out[group, c, p * 4 + 3 : p * 4 + 4, :] = jnp.zeros((1, 256), jnp.float32)
        stat_copy(group, c, way).start()
        part_copy(group, c, way).start()

    def add_incoming(group, c, way):
        stat_copy(group, c, way).wait_recv()
        part_copy(group, c, way).wait_recv()
        slot = group + count * way
        for p in range(2):
            at = p * 4
            there = stat_in[slot, c, at : at + 1, :]
            here = sum_stat[group, c, at : at + 1, :]
            peak = jnp.maximum(here, there)
            keep, add = jnp.exp(here - peak), jnp.exp(there - peak)
            sum_stat[group, c, at : at + 1, :] = peak
            sum_stat[group, c, at + 1 : at + 2, :] = (
                sum_stat[group, c, at + 1 : at + 2, :] * keep
                + stat_in[slot, c, at + 1 : at + 2, :] * add
            )
            part = part_in[slot, c, p].astype(jnp.int32).astype(jnp.float32)
            sums[group, c, p] = sums[group, c, p] * keep + part * (
                add * stat_in[slot, c, at + 2 : at + 3, :]
            )

    def attend(group, c):
        query_now[...] = query_slots[group, c]
        codes = [asked_smem[group, 0, j] for j in range(capacity)]
        slots = [code // 2 for code in codes]
        prompts = [code % 2 for code in codes]
        peaks = [jnp.full((1, 256), LOW, jnp.float32) for _ in range(2)]
        for j in range(capacity):
            key_scale = scale_ref[c, 0, slots[j]] * factor
            part = nt_dot(keys[slots[j], c], query_now[prompts[j]]) * key_scale
            scores[j] = part
            peak = jnp.max(part, axis=0, keepdims=True)
            for p in range(2):
                peaks[p] = jnp.maximum(peaks[p], jnp.where(prompts[j] == p, peak, LOW))
        totals = [jnp.zeros((1, 256), jnp.float32) for _ in range(2)]
        sums[group, c] = jnp.zeros((2, 128, 256), jnp.float32)
        for j in range(capacity):
            peak = jnp.where(prompts[j] == 0, peaks[0], peaks[1])
            grown = jnp.exp(scores[j] - peak)
            total = jnp.sum(grown, axis=0, keepdims=True)
            mixed = jnp.dot(
                values[slots[j], c],
                grown.astype(jnp.bfloat16),
                preferred_element_type=jnp.float32,
            )
            value_scale = scale_ref[c, 1, slots[j]]
            for p in range(2):
                totals[p] = totals[p] + jnp.where(prompts[j] == p, total, 0.0)
                sums[group, c, p] = sums[group, c, p] + mixed * jnp.where(prompts[j] == p, value_scale, 0.0)
        for p in range(2):
            sum_stat[group, c, p * 4 : p * 4 + 1, :] = peaks[p]
            sum_stat[group, c, p * 4 + 1 : p * 4 + 2, :] = totals[p]

    def serve(group, c, way):
        attend(group, c)

        @pl.when(jnp.logical_not(has_next(way)))
        def _():
            code_and_send(group, c, 1 - way)

    def serve_next(index, carry):
        distance, way = 1 + index // 2 % (count - 1), index % 2
        c = index // (2 * (count - 1))
        group = me - (1 - 2 * way) * distance

        @pl.when((group >= 0) & (group < count))
        def _():
            query_copy(group, c, group).wait_recv()
            serve(group, c, way)

        return carry

    def pass_on(c, passed, distance):
        for way in range(2):
            group = me + (1 - 2 * way) * distance
            behind = me if way == 0 else count - 1 - me

            @pl.when((group >= 0) & (group < count) & (behind == passed))
            def _(way=way, group=group):
                add_incoming(group, c, way)
                code_and_send(group, c, way)

    def finish(c):
        for way in range(2):

            @pl.when(has_next(1 - way))
            def _(way=way):
                add_incoming(me, c, way)

        for p in range(2):
            at = p * 4
            here = sum_stat[me, c, at : at + 1, :]
            local_peak = local_stat[c, p, 0:1, :]
            peak = jnp.maximum(here, local_peak)
            keep, add = jnp.exp(here - peak), jnp.exp(local_peak - peak)
            total = keep * sum_stat[me, c, at + 1 : at + 2, :] + add * local_stat[c, p, 1:2, :]
            mixed = sums[me, c, p] * (keep / total) + local_sum[c, p] * (add / total)
            turned[p, c] = mixed.T.reshape(2, 16, 8, 128)

    def attend_own(c, carry):
        attend(me, c)
        return carry

    lax.fori_loop(0, 2, attend_own, 0)
    lax.fori_loop(0, 4 * (count - 1), serve_next, 0)
    for passed in range(1, count - 1):
        for distance in range(1, count - passed):
            for c in range(2):
                pass_on(c, passed, distance)
    finish(0)
    finish(1)
    for p in range(2):
        both = jnp.concatenate([turned[p, 0], turned[p, 1]], axis=2)
        out_ref[:, p * 16 : p * 16 + 16] = both.astype(jnp.bfloat16)

    for other in others:
        ask_copy(me, other).wait_send()
        for c in range(2):
            query_copy(me, c, other).wait_send()
    for c in range(2):
        for way in range(2):
            for distance in range(count):
                target = me + distance if way == 0 else me - distance
                if distance > 0:

                    @pl.when((target >= 0) & (target < count))
                    def _(way=way, target=target, c=c):
                        stat_copy(target, c, way).wait_send()
                        part_copy(target, c, way).wait_send()


def move_queries(
    page_pool, page_scales, queries, new_entries, token_cache, cache_fill, page_counts, page_table
):
    count = lax.axis_size("pre")
    pool_rows = page_pool.shape[0]
    capacity = pool_rows // count
    width = queries.shape[-1]
    vmem = pl.BlockSpec(memory_space=pltpu.VMEM)
    hbm = pl.BlockSpec(memory_space=pltpu.HBM)
    dma = pltpu.SemaphoreType.DMA
    f32, bf16 = jnp.float32, jnp.bfloat16
    return pl.pallas_call(
        functools.partial(attend_kernel, (count, capacity, 1.0 / math.sqrt(width))),
        out_shape=jax.ShapeDtypeStruct(queries.shape, queries.dtype),
        in_specs=[hbm] * 8,
        out_specs=vmem,
        scratch_shapes=[
            pltpu.SMEM(page_counts.shape, jnp.int32),
            pltpu.SMEM(page_table.shape, jnp.int32),
            pltpu.VMEM((2, 2, pool_rows), bf16),
            pltpu.VMEM((2, 2, pool_rows), f32),
            pltpu.SMEM((2, 2, pool_rows), f32),
            pltpu.SMEM(cache_fill.shape, jnp.int32),
            pltpu.VMEM(queries.shape, bf16),
            pltpu.VMEM((512, 128), bf16),
            pltpu.VMEM((256, 128), bf16),
            pltpu.VMEM((count, 1, 128), jnp.int32),
            pltpu.VMEM((pool_rows, 512, 128), bf16),
            pltpu.VMEM((pool_rows, 2, 128, 128), bf16),
            pltpu.VMEM((pool_rows, 2, 128, 128), bf16),
            pltpu.VMEM((count, 1, 128), jnp.int32),
            pltpu.SMEM((count, 1, 128), jnp.int32),
            pltpu.VMEM((count, 2, 2, 256, 128), bf16),
            pltpu.VMEM((2, 256, 128), bf16),
            pltpu.VMEM((capacity, 128, 256), f32),
            pltpu.VMEM((count, 2, 2, 128, 256), f32),
            pltpu.VMEM((count, 2, 8, 256), f32),
            pltpu.VMEM((count, 2, 2, 128, 256), jnp.int16),
            pltpu.VMEM((2 * count, 2, 2, 128, 256), jnp.int16),
            pltpu.VMEM((count, 2, 8, 256), f32),
            pltpu.VMEM((2 * count, 2, 8, 256), f32),
            pltpu.VMEM((2, 2, 128, 256), f32),
            pltpu.VMEM((2, 2, 8, 256), f32),
            pltpu.VMEM((2, 2, 2, 16, 8, 128), f32),
            dma((8,)),
            dma((count,)),
            dma((count,)),
            dma((count,)),
            dma((count, 2)),
            dma((count, 2)),
            dma((count, 2)),
            dma((2 * count, 2)),
            dma((count, 2)),
            dma((2 * count, 2)),
        ],
        compiler_params=pltpu.CompilerParams(
            collective_id=0, has_side_effects=True, vmem_limit_bytes=62 * 1024 * 1024
        ),
    )(
        page_counts,
        page_table,
        page_scales.transpose(1, 2, 0),
        cache_fill,
        queries,
        token_cache.reshape(-1, width),
        new_entries.reshape(-1, width),
        page_pool.reshape(pool_rows, -1, width),
    )


def shards(
    page_pool, page_scales, queries, new_entries, token_cache, cache_fill, page_counts, page_table
):
    args = (
        page_pool, page_scales, queries, new_entries, token_cache, cache_fill, page_counts, page_table,
    )
    count = lax.axis_size("pre")
    capacity = page_pool.shape[0] // count
    if count in (2, 4, 8) and page_pool.shape[0] % (4 * count) == 0 and capacity * page_pool[0].size > 2 * queries.size:
        return move_queries(*args)
    return move_pages(*args)


def solution(mesh):
    in_specs = (
        P(("groups", "pre"), None, "dec", None, None),
        P(("groups", "pre"), "dec", None),
        P(None, ("groups", "pre"), "dec", None),
        P(None, ("groups", "pre"), "dec", None, None),
        P(("groups", "pre"), None, "dec", None, None),
        P(("groups", "pre")),
        P(("groups", "pre"), None),
        P(("groups", "pre"), None, None),
    )
    out_specs = P(None, ("groups", "pre"), "dec", None)
    return jax.shard_map(shards, mesh=mesh, in_specs=in_specs, out_specs=out_specs, check_vma=False)
```
